32 devices in a mesh: groups: 2 (over y), section: 4 (over z), fsdp: 4 (over x, core).
Axes of the slice: x: 2, y: 2, z: 4, core: 2. Of those that a mesh axis runs over, the one named last changes fastest.
Arguments:
- sent_act: bfloat16 [4, 1024, 4096], P('section', 'groups', 'fsdp'), parts along dimension 1, may hold values from -6 to 6
- sent_grad: bfloat16 [4, 1024, 4096], P('section', 'groups', 'fsdp'), parts along dimension 1, may hold values from -6 to 6
- stash_in: bfloat16 [4, 2, 1024, 4096], P('section', None, 'groups', 'fsdp'), parts along dimension 2, may hold values from -6 to 6
- stash_pre: bfloat16 [4, 2, 1024, 4096], P('section', None, 'groups', 'fsdp'), parts along dimension 2, may hold values from -6 to 6
- layer_weight: bfloat16 [4, 4096, 4096], P('section', None, 'fsdp'), may hold values from -0.125 to 0.125
- layer_bias: float32 [4, 4096], P('section', 'fsdp'), may hold values from -3 to 3
- seg_table: bfloat16 [4784, 4096], P('section', 'fsdp'), may hold values from -6 to 6
- seg_index: int32 [1024, 32], P('groups'), parts along dimension 0, may hold values from 0 to 4783
- seg_amp: float32 [1024, 32], P('groups'), parts along dimension 0, may hold values from -1.2 to 1.2
- field_angle: float32 [1024, 2], P('groups'), parts along dimension 0, may hold values from -1 to 1
- angle_weight: float32 [2, 4096], P(None, 'fsdp'), may hold values from -3 to 3
- target: bfloat16 [1024, 4096], P('groups', 'fsdp'), parts along dimension 0, may hold values from -6 to 6
- sched: int32 [4], P('section'), may hold values from 0 to 1
Outputs:
- fwd_out: bfloat16 [4, 1024, 4096], P('section', 'groups', 'fsdp'), parts along dimension 1
- grad_in: bfloat16 [4, 1024, 4096], P('section', 'groups', 'fsdp'), parts along dimension 1
- grad_w: bfloat16 [4, 8192, 4096], P('section', 'groups', 'fsdp'), parts along dimension 1
- grad_bias: float32 [4, 8192], P('section', ('groups', 'fsdp')), parts along dimension 1
The draws below stay inside these ranges and needn't reach their ends.
There are 2 independent parts, one for each index of `groups`. The reference program is written for one: setup_inputs(seed, part) draws one part's arguments, and reference() takes and returns one part's arrays. A program takes and returns all parts, laid end to end along the dimension named above; an argument that names none is the same for every part. Nothing has to cross between parts.
All inputs are finite; a program needn't handle non-finite values.
Results may differ from the reference program's by a relative error of at most 0.017.
Values may be sent and summed in bfloat16 or wider, within the bound.
A program may use at most 128 MiB of HBM per device.

```python
import jax
import jax.numpy as jnp
from jax import lax

D = 4096
NSEG = 4784
KACT = 32
MB = 512
NSTASH = 2
N_SECTION = 4
N_FSDP = 4


def draw_sched(key, part):
    offset = jax.random.randint(key, (), 0, NSTASH)
    return jnp.mod(jnp.arange(N_SECTION, dtype=jnp.int32) + offset, NSTASH).astype(jnp.int32)


def draw_sent_grad(key, part):
    noise_key = jax.random.fold_in(key, 11)
    column_key = jax.random.fold_in(key, 12)
    noise = jax.random.normal(noise_key, (N_SECTION, MB, D), jnp.float32)
    column = 0.5 * jax.random.normal(column_key, (N_SECTION, 1, D), jnp.float32)
    return jnp.clip(noise + column, -6.0, 6.0).astype(jnp.bfloat16)


def with_ends(entries, stream_key, least, top_value):
    longest = entries.shape.index(max(entries.shape))
    spots = []
    for shift in (0, 1):
        where = [jax.random.randint(jax.random.fold_in(stream_key, axis), (), 0, length) for axis, length in enumerate(entries.shape)]
        where[longest] = (where[longest] + shift) % entries.shape[longest]
        spots.append(tuple(where))
    return entries.at[spots[0]].set(least).at[spots[1]].set(top_value)


def strengthened(array, own_key, source, target, parts, factor):
    owner, partner = [(jnp.arange(array.shape[dim]) // (array.shape[dim] // parts)).reshape([-1 if axis == dim else 1 for axis in range(array.ndim)]) for dim in (source, target)]
    chosen = jax.random.permutation(own_key, parts)[partner]
    strong = (owner == chosen) | (owner == (partner + parts // 2) % parts)
    return jnp.where(strong, factor * array, array)


def block_levels(key, extent, shards, smallest, high):
    def one(position, blocks):
        steps = jax.random.uniform(jax.random.fold_in(jax.random.fold_in(key, 6), position), (blocks,), jnp.float32, smallest / len(shards), high / len(shards))
        return jnp.repeat(jnp.exp(steps), extent[position] // blocks).reshape((-1,) + (1,) * (len(extent) - position - 1))

    factor_of = one(*shards[0])
    for cut in shards[1:]:
        factor_of = factor_of * one(*cut)
    return factor_of


def bell_draw(key, dims, scale, reach, pieces=(), kind=jnp.bfloat16):
    values = scale * jax.random.normal(key, dims, jnp.float32)
    if pieces:
        values = values * block_levels(key, dims, pieces, -0.22, 0.18)
    return jnp.clip(values, -reach, reach).astype(kind)


def noise_with(rng, extent, scale, bound, shards, heavy, kind=jnp.bfloat16):
    array = scale * jax.random.normal(rng, extent, jnp.float32)
    if shards:
        array = array * block_levels(rng, extent, shards, -0.22, 0.18)
    return jnp.clip(strengthened(array, jax.random.fold_in(rng, 3), *heavy), -bound, bound).astype(kind)


def setup_inputs(seed: int = 0, part: int = 0) -> dict:
    splits = jax.random.split(jax.random.key(seed), 14)
    part_splits = jax.random.split(jax.random.fold_in(splits[13], part), 14)
    return {
        "sent_act": bell_draw(part_splits[0], (N_SECTION, MB, D), 1.0, 6.0, ((0, 4), (2, 4))),
        "sent_grad": draw_sent_grad(jax.random.fold_in(jax.random.fold_in(splits[13], part), 71), part),
        "stash_in": bell_draw(part_splits[2], (N_SECTION, NSTASH, MB, D), 1.0, 6.0, ((0, 4), (3, 4))),
        "stash_pre": bell_draw(part_splits[3], (N_SECTION, NSTASH, MB, D), 1.0, 6.0, ((0, 4), (3, 4))),
        "layer_weight": noise_with(splits[4], (N_SECTION, D, D), D ** -0.5, 0.125, ((0, 4), (2, 4)), (2, 1, 4, 2.0)),
        "layer_bias": bell_draw(splits[5], (N_SECTION, D), 0.5, 3.0, ((0, 4), (1, 4)), jnp.float32),
        "seg_table": bell_draw(splits[6], (NSEG, D), 1.0, 6.0, ((0, 4), (1, 4))),
        "seg_index": with_ends(jax.random.randint(part_splits[7], (MB, KACT), 0, NSEG), jax.random.fold_in(part_splits[7], 1), 0, NSEG - 1).astype(jnp.int32),
        "seg_amp": bell_draw(part_splits[8], (MB, KACT), 0.2, 1.2, (), jnp.float32),
        "field_angle": jnp.clip(jax.random.uniform(part_splits[9], (MB, 2), jnp.float32, -1.0, 1.0), -1.0, 1.0),
        "angle_weight": bell_draw(splits[10], (2, D), 0.5, 3.0, ((1, 4),), jnp.float32),
        "target": bell_draw(part_splits[11], (MB, D), 1.0, 6.0, ((1, 4),)),
        "sched": draw_sched(jax.random.fold_in(splits[13], 71), part),
    }


def gelu_back(stashed_pre, target_rows, cotangent_in, is_last):
    stashed_f32 = stashed_pre.astype(jnp.float32)
    stashed_act, pullback = jax.vjp(jax.nn.gelu, stashed_f32)
    if is_last:
        cotangent = stashed_act - target_rows.astype(jnp.float32)
    else:
        cotangent = cotangent_in.astype(jnp.float32)
    return pullback(cotangent)[0].astype(jnp.bfloat16)

def reference(sent_act, sent_grad, stash_in, stash_pre, layer_weight, layer_bias, seg_table, seg_index, seg_amp, field_angle, angle_weight, target, sched):
    embedded = jnp.zeros((MB, D), jnp.float32)
    for column in range(KACT):
        picked = jnp.take(seg_table, seg_index[:, column], axis=0).astype(jnp.float32)
        embedded = embedded + seg_amp[:, column:column + 1] * picked
    angular = jnp.dot(field_angle, angle_weight, precision=lax.Precision.HIGHEST)
    first_input = (embedded + angular).astype(jnp.bfloat16)
    width = D // N_FSDP
    outputs, input_grads, weight_grads, bias_grads = ([], [], [], [])
    for section_num in range(N_SECTION):
        layer_input = first_input if section_num == 0 else sent_act[section_num - 1]
        preact = jnp.dot(layer_input, layer_weight[section_num], preferred_element_type=jnp.float32) + layer_bias[section_num]
        outputs.append(jax.nn.gelu(preact).astype(jnp.bfloat16))
        stash_slot = sched[section_num]
        stashed_in = stash_in[section_num][stash_slot]
        stashed_pre = stash_pre[section_num][stash_slot]
        following = sent_grad[min(section_num + 1, N_SECTION - 1)]
        pre_grad = gelu_back(stashed_pre, target, following, section_num == N_SECTION - 1)
        weight_grads.append(jnp.dot(stashed_in.T, pre_grad, preferred_element_type=jnp.float32).astype(jnp.bfloat16))
        bias_grads.append(lax.optimization_barrier(jnp.sum(pre_grad.astype(jnp.float32), axis=0)))
        summed = jnp.zeros((MB, D), jnp.float32)
        for shard_num in range(N_FSDP):
            lower = shard_num * width
            input_part = jnp.dot(pre_grad[:, lower:lower + width], layer_weight[section_num][:, lower:lower + width].T, preferred_element_type=jnp.float32).astype(jnp.bfloat16)
            summed = summed + input_part.astype(jnp.float32)
        input_grads.append(summed.astype(jnp.bfloat16))
    return (jnp.stack(outputs), jnp.stack(input_grads), jnp.stack(weight_grads), jnp.stack(bias_grads))
```

```python
import functools

import jax
import jax.numpy as jnp
from jax import lax
from jax.experimental import pallas as pl
from jax.experimental.pallas import tpu as pltpu
from jax.sharding import PartitionSpec as P

CHUNKS = 4
MESH = pl.DeviceIdType.MESH
ROOT = 0.7978845608028654
CUBIC = 0.044715


def gelu_parts(x):
    squared = x * x
    t = jnp.tanh(ROOT * (x + CUBIC * x * squared))
    half = 0.5 * (1.0 + t)
    slope = half + 0.5 * x * (1.0 - t * t) * (ROOT * (1.0 + 3.0 * CUBIC * squared))
    return x * half, slope


def gelu(x):
    return x * (0.5 * (1.0 + jnp.tanh(ROOT * (x + CUBIC * x * x * x))))


def kernel(
    sections, shards,
    act_hbm, grad_hbm, stash_hbm, pre_hbm, weight_hbm, bias_hbm, table_hbm, index_hbm, amp_hbm,
    field_hbm, angle_hbm, target_hbm, sched_ref,
    fwd_ref, grad_in_ref, grad_w_ref, grad_bias_ref,
    stash_ref, pre_ref, weight, bias_ref, table_ref, index_ref, amp_ref, field_ref, angle_ref, target_ref,
    ids, amps, fields,
    feat, stash, from_next, matrix, emb, emb_recv, emb_send, pre_grad,
    part_send, part_recv, own, x_recv,
    stash_sem, load_sem, z_send, z_recv, near_send, near_recv, far_send, far_recv, pass_send, pass_recv,
    part_send_sem, part_recv_sem, sum_send_sem, sum_recv_sem,
):
    me = lax.axis_index("fsdp")
    sec = lax.axis_index("section")
    chips = shards // 2
    chip, core = me // 2, lax.rem(me, 2)
    partner = chip * 2 + 1 - core
    rows, width = pre_grad.shape
    part = rows // CHUNKS
    tile = min(256, width)

    def at_chip(j, c):
        return lax.rem(chip + j, chips) * 2 + c

    def span(c):
        return pl.ds(c * part, part)

    def moving(c):
        return pl.ds(pl.multiple_of(c * part, part), part)

    def remote(src, dst, send, recv, **where):
        return pltpu.make_async_remote_copy(
            src_ref=src, dst_ref=dst, send_sem=send, recv_sem=recv,
            device_id=where, device_id_type=MESH,
        )

    not_last = sec < sections - 1
    not_first = sec > 0

    def stash_load(c):
        return pltpu.make_async_copy(stash_hbm.at[0, :, span(c)], stash_ref.at[:, span(c)], stash_sem.at[c])

    loads = {
        name: pltpu.make_async_copy(src, dst, load_sem.at[k])
        for k, (name, src, dst) in enumerate([
            ("index", index_hbm, index_ref),
            ("amp", amp_hbm, amp_ref),
            ("table", table_hbm, table_ref),
            ("pre", pre_hbm.at[0], pre_ref),
            ("target", target_hbm, target_ref),
            ("weight", weight_hbm.at[0], weight),
            ("bias", bias_hbm, bias_ref),
            ("field", field_hbm, field_ref),
            ("angle", angle_hbm, angle_ref),
        ])
    }
    for c in range(CHUNKS):
        stash_load(c).start()

    barrier = pltpu.get_barrier_semaphore()
    pl.semaphore_signal(barrier, inc=1, device_id={"fsdp": partner}, device_id_type=MESH)
    for j in range(1, chips):
        pl.semaphore_signal(barrier, inc=1, device_id={"fsdp": at_chip(j, core)}, device_id_type=MESH)

    @pl.when(not_last)
    def _():
        pl.semaphore_signal(barrier, inc=1, device_id={"section": sec + 1}, device_id_type=MESH)

    @pl.when(not_first)
    def _():
        pl.semaphore_signal(barrier, inc=1, device_id={"section": sec - 1}, device_id_type=MESH)

    for copy in loads.values():
        copy.start()

    pl.semaphore_wait(barrier, chips + jnp.where(not_last, 1, 0) + jnp.where(not_first, 1, 0))

    def act_copy(c):
        return remote(act_hbm.at[0, moving(c)], feat.at[me, moving(c)], z_send.at[0, c], z_recv.at[0, c], section=sec + 1)

    def grad_copy(c):
        return remote(grad_hbm.at[0, moving(c)], from_next.at[moving(c)], z_send.at[1, c], z_recv.at[1, c], section=sec - 1)

    def emb_copy(c):
        return remote(emb_send.at[moving(c)], emb_recv.at[moving(c)], z_send.at[2, c], z_recv.at[2, c], section=sec - 1)

    @pl.when(not_first)
    def _():
        for c in range(CHUNKS):
            grad_copy(c).start()

    @pl.when(not_last)
    def _():
        for c in range(CHUNKS):
            act_copy(c).start()

    def near_copy(g, buf, c, block):
        return remote(buf.at[block, moving(c)], buf.at[block, moving(c)], near_send.at[g, c], near_recv.at[g, c], fsdp=partner)

    def far_copy(g, buf, c, j, block):
        return remote(buf.at[block, moving(c)], buf.at[block, moving(c)], far_send.at[g, c, j - 1], far_recv.at[g, c, j - 1], fsdp=at_chip(j, core))

    def pass_copy(g, buf, c, j, block):
        return remote(buf.at[block, moving(c)], buf.at[block, moving(c)], pass_send.at[g, c, j - 1], pass_recv.at[g, c, j - 1], fsdp=partner)

    def gather_start(g, buf, c):
        for j in range(1, chips):
            far_copy(g, buf, c, j, me).start()
        near_copy(g, buf, c, me).start()

    def gather_pass(g, buf, c):
        for j in range(1, chips):
            block = at_chip(chips - j, core)
            far_copy(g, buf, c, j, block).wait_recv()
            pass_copy(g, buf, c, j, block).start()

    def gather_end(g, buf, c):
        near_copy(g, buf, c, partner).wait_recv()
        for j in range(1, chips):
            pass_copy(g, buf, c, j, at_chip(chips - j, 1 - core)).wait_recv()

    def gather_drain(g, buf, c):
        near_copy(g, buf, c, me).wait_send()
        for j in range(1, chips):
            far_copy(g, buf, c, j, me).wait_send()
            pass_copy(g, buf, c, j, at_chip(chips - j, core)).wait_send()

    slot = sched_ref[0]
    for c in range(CHUNKS):
        stash_load(c).wait()
        stash[me, span(c), :] = jnp.where(slot == 0, stash_ref[0, span(c), :], stash_ref[1, span(c), :])
        gather_start(0, stash, c)

    table_rows = table_ref.shape[0]
    wide = matrix.shape[1]
    base = sec * table_rows

    for name in ("index", "amp", "field", "angle", "table"):
        loads[name].wait()
    ids[...] = index_ref[...].T
    amps[...] = amp_ref[...].T
    fields[...] = jnp.concatenate([field_ref[...], jnp.zeros((6, rows), jnp.float32)], axis=0).T

    def amplitudes(i, carry):
        at = pl.ds(pl.multiple_of(i * 16, 16), 16)
        names = ids[at, :]
        weights = amps[at, :]
        position = lax.broadcasted_iota(jnp.int32, (16, wide), 1) + base
        total = jnp.zeros((16, wide), jnp.float32)
        for k in range(names.shape[1]):
            total = total + jnp.where(names[:, k : k + 1] == position, weights[:, k : k + 1], 0.0)
        matrix[at, :] = total.astype(jnp.bfloat16)
        return carry

    def embed(c, carry):
        lax.fori_loop(c * (part // 16), (c + 1) * (part // 16), amplitudes, 0)
        emb[moving(c), :] = jnp.dot(
            matrix[moving(c), :table_rows], table_ref[...], preferred_element_type=jnp.float32
        )

        @pl.when(jnp.logical_not(not_last))
        def _():
            emb_send[moving(c), :] = emb[moving(c), :].astype(jnp.bfloat16)
            emb_copy(c).start()

        return carry

    lax.fori_loop(0, CHUNKS, embed, 0)

    def input_part(j, c, into, r):
        block = at_chip(j, c)
        for t in range(width // tile):
            begin = pl.multiple_of(block * width + t * tile, tile)
            into[j, moving(r), t * tile : (t + 1) * tile] = lax.dot_general(
                pre_grad[moving(r), :], weight[pl.ds(begin, tile), :], (((1,), (1,)), ((), ())),
                preferred_element_type=jnp.float32,
            ).astype(jnp.bfloat16)

    def part_copy(j, c):
        return remote(part_send.at[j, moving(c)], part_recv.at[j, moving(c)], part_send_sem.at[j, c], part_recv_sem.at[j, c], fsdp=partner)

    def sum_copy(j, c):
        return remote(own.at[j, moving(c)], x_recv.at[j - 1, moving(c)], sum_send_sem.at[j - 1, c], sum_recv_sem.at[j - 1, c], fsdp=at_chip(j, core))

    for name in ("pre", "target", "weight", "bias"):
        loads[name].wait()
    grad_bias_ref[...] = jnp.zeros_like(grad_bias_ref)

    def backward(c, carry):
        @pl.when(not_last)
        def _():
            grad_copy(c).wait_recv()

        def step(i, carry):
            at = pl.ds(pl.multiple_of(c * part + i * 16, 16), 16)
            saved = jnp.where(slot == 0, pre_ref[0, at, :], pre_ref[1, at, :]).astype(jnp.float32)
            value, slope = gelu_parts(saved)
            cotangent = jnp.where(
                not_last, from_next[at, :].astype(jnp.float32), value - target_ref[at, :].astype(jnp.float32)
            )
            result = (cotangent * slope).astype(jnp.bfloat16)
            pre_grad[at, :] = result
            grad_bias_ref[...] += jnp.sum(result.astype(jnp.float32), axis=0, keepdims=True)
            return carry

        lax.fori_loop(0, part // 16, step, 0)

        for j in list(range(1, chips)) + [0]:
            input_part(j, 1 - core, part_send, c)
            part_copy(j, c).start()

        @pl.when(not_first)
        def _():
            act_copy(c).wait_recv()
            gather_start(1, feat, c)

        for j in list(range(1, chips)) + [0]:
            input_part(j, core, own, c)
        for j in range(1, chips):
            part_copy(j, c).wait_recv()
            own[j, moving(c), :] = (
                own[j, moving(c), :].astype(jnp.float32) + part_recv[j, moving(c), :].astype(jnp.float32)
            ).astype(jnp.bfloat16)
            sum_copy(j, c).start()
        return carry

    lax.fori_loop(0, CHUNKS, backward, 0)

    def chain(c):
        @pl.when(not_last)
        def _():
            emb_copy(c).wait_recv()

            def add(i, carry):
                at = pl.ds(pl.multiple_of(c * part + i * 16, 16), 16)
                total = emb[at, :] + emb_recv[at, :].astype(jnp.float32)

                @pl.when(not_first)
                def _():
                    emb_send[at, :] = total.astype(jnp.bfloat16)

                @pl.when(sec == 0)
                def _():
                    angular = (
                        fields[at, 0:1] * angle_ref[0:1, :] + fields[at, 1:2] * angle_ref[1:2, :]
                    )
                    feat[me, at, :] = (total + angular).astype(jnp.bfloat16)

                return carry

            lax.fori_loop(0, part // 16, add, 0)

            @pl.when(not_first)
            def _():
                emb_copy(c).start()

            @pl.when(sec == 0)
            def _():
                gather_start(1, feat, c)

    def weight_grad(block):
        def step(t, carry):
            begin = pl.multiple_of(block * width + t * tile, tile)
            column = pl.ds(pl.multiple_of(t * tile, tile), tile)
            grad_w_ref[0, pl.ds(begin, tile), :] = lax.dot_general(
                stash[block, :, column], pre_grad[...], (((0,), (0,)), ((), ())),
                preferred_element_type=jnp.float32,
            ).astype(jnp.bfloat16)
            return carry

        lax.fori_loop(0, width // tile, step, 0)

    blocks = [me, partner]
    for j in range(1, chips):
        blocks += [at_chip(j, core), at_chip(j, 1 - core)]
    weight_grad(blocks[0])
    for c in range(CHUNKS):
        gather_pass(0, stash, c)
    for c in range(CHUNKS):
        chain(c)
        if c == 0:
            for r in range(CHUNKS):
                gather_end(0, stash, r)
        for b in blocks[1 + c * (shards - 1) // CHUNKS : 1 + (c + 1) * (shards - 1) // CHUNKS]:
            weight_grad(b)

    def forward(c, carry):
        gather_pass(1, feat, c)
        for j in range(1, chips):
            sum_copy(j, c).wait_recv()
        part_copy(0, c).wait_recv()
        whole = own[0, moving(c), :].astype(jnp.float32) + part_recv[0, moving(c), :].astype(jnp.float32)
        for j in range(1, chips):
            whole = whole + x_recv[j - 1, moving(c), :].astype(jnp.float32)
        grad_in_ref[0, moving(c), :] = whole.astype(jnp.bfloat16)
        gather_end(1, feat, c)
        total = jnp.zeros((part, width), jnp.float32)
        for b in range(shards):
            total = total + jnp.dot(
                feat[b, moving(c), :], weight[b * width : (b + 1) * width, :],
                preferred_element_type=jnp.float32,
            )
        fwd_ref[0, moving(c), :] = gelu(total + bias_ref[...]).astype(jnp.bfloat16)
        return carry

    lax.fori_loop(0, CHUNKS, forward, 0)

    for c in range(CHUNKS):
        gather_drain(0, stash, c)
        gather_drain(1, feat, c)
        for j in range(chips):
            part_copy(j, c).wait_send()
        for j in range(1, chips):
            sum_copy(j, c).wait_send()

    @pl.when(not_last)
    def _():
        for c in range(CHUNKS):
            act_copy(c).wait_send()

    @pl.when(not_first)
    def _():
        for c in range(CHUNKS):
            grad_copy(c).wait_send()
            emb_copy(c).wait_send()


def store(pieces, fwd, grad_in, grad_w, grad_bias, fwd_out, grad_in_out, grad_w_out, grad_bias_out, sem):
    depth = grad_w.shape[1] // pieces
    copies = [(grad_w.at[0, pl.ds(i * depth, depth)], grad_w_out.at[0, pl.ds(i * depth, depth)]) for i in range(pieces)]
    copies += [(fwd, fwd_out), (grad_in, grad_in_out), (grad_bias, grad_bias_out)]
    copies = [pltpu.make_async_copy(src, dst, sem.at[i]) for i, (src, dst) in enumerate(copies)]
    for copy in copies:
        copy.start()
    for copy in copies:
        copy.wait()


def local(sections, shards, *args):
    args = list(args)
    rows, width = args[0].shape[1:]
    table_rows = args[6].shape[0]
    active = args[7].shape[1]
    for k in (7, 8, 9):
        args[k] = args[k].T
    wide = (table_rows + 127) // 128 * 128
    chips = shards // 2
    vmem = pl.BlockSpec(memory_space=pltpu.VMEM)
    hbm = pl.BlockSpec(memory_space=pltpu.HBM)
    smem = pl.BlockSpec(memory_space=pltpu.SMEM)
    dma = pltpu.SemaphoreType.DMA
    half, full = jnp.bfloat16, jnp.float32
    outs = (
        ((1, rows, width), half),
        ((1, rows, width), half),
        ((1, shards * width, width), half),
        ((1, width), full),
    )
    results = pl.pallas_call(
        functools.partial(kernel, sections, shards),
        out_shape=tuple(pltpu.VMEM(*out) for out in outs),
        in_specs=[hbm] * 12 + [smem],
        out_specs=(vmem,) * 4,
        scratch_shapes=[
            pltpu.VMEM((2, rows, width), half),
            pltpu.VMEM((2, rows, width), half),
            pltpu.VMEM((shards * width, width), half),
            pltpu.VMEM((1, width), full),
            pltpu.VMEM((table_rows, width), half),
            pltpu.VMEM((active, rows), jnp.int32),
            pltpu.VMEM((active, rows), full),
            pltpu.VMEM((2, rows), full),
            pltpu.VMEM((2, width), full),
            pltpu.VMEM((rows, width), half),
            pltpu.VMEM((rows, active), jnp.int32),
            pltpu.VMEM((rows, active), full),
            pltpu.VMEM((rows, 8), full),
            pltpu.VMEM((shards, rows, width), half),
            pltpu.VMEM((shards, rows, width), half),
            pltpu.VMEM((rows, width), half),
            pltpu.VMEM((rows, wide), half),
            pltpu.VMEM((rows, width), full),
            pltpu.VMEM((rows, width), half),
            pltpu.VMEM((rows, width), half),
            pltpu.VMEM((rows, width), half),
            pltpu.VMEM((chips, rows, width), half),
            pltpu.VMEM((chips, rows, width), half),
            pltpu.VMEM((chips, rows, width), half),
            pltpu.VMEM((chips - 1, rows, width), half),
            dma((CHUNKS,)),
            dma((9,)),
            dma((3, CHUNKS)),
            dma((3, CHUNKS)),
            dma((2, CHUNKS)),
            dma((2, CHUNKS)),
            dma((2, CHUNKS, chips - 1)),
            dma((2, CHUNKS, chips - 1)),
            dma((2, CHUNKS, chips - 1)),
            dma((2, CHUNKS, chips - 1)),
            dma((chips, CHUNKS)),
            dma((chips, CHUNKS)),
            dma((chips - 1, CHUNKS)),
            dma((chips - 1, CHUNKS)),
        ],
        compiler_params=pltpu.CompilerParams(
            collective_id=0, has_side_effects=True, vmem_limit_bytes=46 * 1024 * 1024
        ),
        cost_estimate=pl.CostEstimate(
            flops=6 * rows * shards * width * width, bytes_accessed=40 * rows * width, transcendentals=0
        ),
    )(*args)
    any_spec = pl.BlockSpec(memory_space=pl.ANY)
    return pl.pallas_call(
        functools.partial(store, 8),
        out_shape=tuple(jax.ShapeDtypeStruct(*out) for out in outs),
        in_specs=[any_spec] * 4,
        out_specs=(any_spec,) * 4,
        scratch_shapes=[dma((11,))],
        compiler_params=pltpu.CompilerParams(vmem_limit_bytes=1024 * 1024),
    )(*results)


def solution(mesh):
    return jax.shard_map(
        functools.partial(local, mesh.shape["section"], mesh.shape["fsdp"]),
        mesh=mesh,
        in_specs=(
            P("section", "groups", "fsdp"),
            P("section", "groups", "fsdp"),
            P("section", None, "groups", "fsdp"),
            P("section", None, "groups", "fsdp"),
            P("section", None, "fsdp"),
            P("section", "fsdp"),
            P("section", "fsdp"),
            P("groups", None),
            P("groups", None),
            P("groups", None),
            P(None, "fsdp"),
            P("groups", "fsdp"),
            P("section"),
        ),
        out_specs=(
            P("section", "groups", "fsdp"),
            P("section", "groups", "fsdp"),
            P("section", "groups", "fsdp"),
            P("section", ("groups", "fsdp")),
        ),
        check_vma=False,
    )
```

```python
import functools

import jax
import jax.numpy as jnp
from jax import lax
from jax.experimental import pallas as pl
from jax.experimental.pallas import tpu as pltpu
from jax.sharding import PartitionSpec as P

CHUNKS = 4
MESH = pl.DeviceIdType.MESH
ROOT = 0.7978845608028654
CUBIC = 0.044715


def gelu_parts(x):
    squared = x * x
    t = jnp.tanh(ROOT * (x + CUBIC * x * squared))
    half = 0.5 * (1.0 + t)
    slope = half + 0.5 * x * (1.0 - t * t) * (ROOT * (1.0 + 3.0 * CUBIC * squared))
    return x * half, slope


def gelu(x):
    return x * (0.5 * (1.0 + jnp.tanh(ROOT * (x + CUBIC * x * x * x))))


def kernel(
    sections, shards,
    act_hbm, grad_hbm, stash_hbm, pre_hbm, weight_hbm, bias_hbm, table_hbm, index_hbm, amp_hbm,
    field_hbm, angle_hbm, target_hbm, sched_ref,
    fwd_ref, grad_in_ref, grad_w_ref, grad_bias_ref,
    stash_ref, pre_ref, weight, bias_ref, table_ref, index_ref, amp_ref, field_ref, angle_ref, target_ref,
    ids, amps, fields,
    feat, stash, from_next, matrix, emb, emb_recv, emb_send, pre_grad,
    part_send, part_recv, own, x_recv,
    stash_sem, load_sem, z_send, z_recv, near_send, near_recv, far_send, far_recv, pass_send, pass_recv,
    part_send_sem, part_recv_sem, sum_send_sem, sum_recv_sem,
):
    me = lax.axis_index("fsdp")
    sec = lax.axis_index("section")
    chips = shards // 2
    chip, core = me // 2, lax.rem(me, 2)
    partner = chip * 2 + 1 - core
    rows, width = pre_grad.shape
    part = rows // CHUNKS
    tile = min(256, width)

    def at_chip(j, c):
        return lax.rem(chip + j, chips) * 2 + c

    def span(c):
        return pl.ds(c * part, part)

    def moving(c):
        return pl.ds(pl.multiple_of(c * part, part), part)

    def remote(src, dst, send, recv, **where):
        return pltpu.make_async_remote_copy(
            src_ref=src, dst_ref=dst, send_sem=send, recv_sem=recv,
            device_id=where, device_id_type=MESH,
        )

    not_last = sec < sections - 1
    not_first = sec > 0

    def stash_load(c):
        return pltpu.make_async_copy(stash_hbm.at[0, :, span(c)], stash_ref.at[:, span(c)], stash_sem.at[c])

    loads = {
        name: pltpu.make_async_copy(src, dst, load_sem.at[k])
        for k, (name, src, dst) in enumerate([
            ("index", index_hbm, index_ref),
            ("amp", amp_hbm, amp_ref),
            ("table", table_hbm, table_ref),
            ("pre", pre_hbm.at[0], pre_ref),
            ("target", target_hbm, target_ref),
            ("weight", weight_hbm.at[0], weight),
            ("bias", bias_hbm, bias_ref),
            ("field", field_hbm, field_ref),
            ("angle", angle_hbm, angle_ref),
        ])
    }
    for c in range(CHUNKS):
        stash_load(c).start()

    barrier = pltpu.get_barrier_semaphore()
    pl.semaphore_signal(barrier, inc=1, device_id={"fsdp": partner}, device_id_type=MESH)
    for j in range(1, chips):
        pl.semaphore_signal(barrier, inc=1, device_id={"fsdp": at_chip(j, core)}, device_id_type=MESH)

    @pl.when(not_last)
    def _():
        pl.semaphore_signal(barrier, inc=1, device_id={"section": sec + 1}, device_id_type=MESH)

    @pl.when(not_first)
    def _():
        pl.semaphore_signal(barrier, inc=1, device_id={"section": sec - 1}, device_id_type=MESH)

    for copy in loads.values():
        copy.start()

    pl.semaphore_wait(barrier, chips + jnp.where(not_last, 1, 0) + jnp.where(not_first, 1, 0))

    def act_copy(c):
        return remote(act_hbm.at[0, moving(c)], feat.at[me, moving(c)], z_send.at[0, c], z_recv.at[0, c], section=sec + 1)

    def grad_copy(c):
        return remote(grad_hbm.at[0, moving(c)], from_next.at[moving(c)], z_send.at[1, c], z_recv.at[1, c], section=sec - 1)

    def emb_copy(c):
        return remote(emb_send.at[moving(c)], emb_recv.at[moving(c)], z_send.at[2, c], z_recv.at[2, c], section=sec - 1)

    @pl.when(not_first)
    def _():
        for c in range(CHUNKS // 2):
            grad_copy(c).start()

    @pl.when(not_first & not_last)
    def _():
        for c in range(CHUNKS // 2, CHUNKS):
            grad_copy(c).start()

    @pl.when(not_last)
    def _():
        for c in range(CHUNKS):
            act_copy(c).start()

    def near_copy(g, buf, c, block):
        return remote(buf.at[block, moving(c)], buf.at[block, moving(c)], near_send.at[g, c], near_recv.at[g, c], fsdp=partner)

    def far_copy(g, buf, c, j, block):
        return remote(buf.at[block, moving(c)], buf.at[block, moving(c)], far_send.at[g, c, j - 1], far_recv.at[g, c, j - 1], fsdp=at_chip(j, core))

    def pass_copy(g, buf, c, j, block):
        return remote(buf.at[block, moving(c)], buf.at[block, moving(c)], pass_send.at[g, c, j - 1], pass_recv.at[g, c, j - 1], fsdp=partner)

    def gather_start(g, buf, c):
        for j in range(1, chips):
            far_copy(g, buf, c, j, me).start()
        near_copy(g, buf, c, me).start()

    def gather_pass(g, buf, c):
        for j in range(1, chips):
            block = at_chip(chips - j, core)
            far_copy(g, buf, c, j, block).wait_recv()
            pass_copy(g, buf, c, j, block).start()

    def gather_end(g, buf, c):
        near_copy(g, buf, c, partner).wait_recv()
        for j in range(1, chips):
            pass_copy(g, buf, c, j, at_chip(chips - j, 1 - core)).wait_recv()

    def gather_drain(g, buf, c):
        near_copy(g, buf, c, me).wait_send()
        for j in range(1, chips):
            far_copy(g, buf, c, j, me).wait_send()
            pass_copy(g, buf, c, j, at_chip(chips - j, core)).wait_send()

    slot = sched_ref[0]
    for c in range(CHUNKS):
        stash_load(c).wait()
        stash[me, span(c), :] = jnp.where(slot == 0, stash_ref[0, span(c), :], stash_ref[1, span(c), :])
        gather_start(0, stash, c)

    table_rows = table_ref.shape[0]
    wide = matrix.shape[1]
    base = sec * table_rows

    for name in ("index", "amp", "field", "angle", "table"):
        loads[name].wait()
    ids[...] = index_ref[...].T
    amps[...] = amp_ref[...].T
    fields[...] = jnp.concatenate([field_ref[...], jnp.zeros((6, rows), jnp.float32)], axis=0).T

    def amplitudes(i, carry):
        at = pl.ds(pl.multiple_of(i * 32, 32), 32)
        names = ids[at, :]
        weights = amps[at, :]
        position = lax.broadcasted_iota(jnp.int32, (32, wide), 1) + base
        total = jnp.zeros((32, wide), jnp.float32)
        for k in range(names.shape[1]):
            total = total + jnp.where(names[:, k : k + 1] == position, weights[:, k : k + 1], 0.0)
        matrix[at, :] = total.astype(jnp.bfloat16)
        return carry

    def embed(c, carry):
        lax.fori_loop(c * (part // 32), (c + 1) * (part // 32), amplitudes, 0)
        emb[moving(c), :] = jnp.dot(
            matrix[moving(c), :table_rows], table_ref[...], preferred_element_type=jnp.float32
        )

        @pl.when(jnp.logical_not(not_last))
        def _():
            emb_send[moving(c), :] = emb[moving(c), :].astype(jnp.bfloat16)
            emb_copy(c).start()

        return carry

    lax.fori_loop(0, CHUNKS, embed, 0)

    @pl.when(jnp.logical_not(not_last))
    def _():
        for c in range(CHUNKS // 2, CHUNKS):
            grad_copy(c).start()

    deep = rows // 2

    def side(h):
        return pl.ds(h * deep, deep)

    def input_part(j, c, into, h):
        block = at_chip(j, c)
        for t in range(width // tile):
            begin = pl.multiple_of(block * width + t * tile, tile)
            into[j, side(h), t * tile : (t + 1) * tile] = lax.dot_general(
                pre_grad[side(h), :], weight[pl.ds(begin, tile), :], (((1,), (1,)), ((), ())),
                preferred_element_type=jnp.float32,
            ).astype(jnp.bfloat16)

    def part_copy(j, h):
        return remote(part_send.at[j, side(h)], part_recv.at[j, side(h)], part_send_sem.at[j, h], part_recv_sem.at[j, h], fsdp=partner)

    def sum_copy(j, c):
        return remote(own.at[j, moving(c)], x_recv.at[j - 1, moving(c)], sum_send_sem.at[j - 1, c], sum_recv_sem.at[j - 1, c], fsdp=at_chip(j, core))

    for name in ("pre", "target", "weight", "bias"):
        loads[name].wait()
    grad_bias_ref[...] = jnp.zeros_like(grad_bias_ref)

    def feed(c):
        @pl.when(not_first)
        def _():
            act_copy(c).wait_recv()
            gather_start(1, feat, c)

    def last_sums():
        for j in range(1, chips):
            sum_copy(j, CHUNKS - 1).start()

    def backward(h):
        first = h * CHUNKS // 2

        def piece(c, carry):
            @pl.when(not_last)
            def _():
                grad_copy(c).wait_recv()

            def step(i, carry):
                at = pl.ds(pl.multiple_of(c * part + i * 16, 16), 16)
                saved = jnp.where(slot == 0, pre_ref[0, at, :], pre_ref[1, at, :]).astype(jnp.float32)
                value, slope = gelu_parts(saved)
                cotangent = jnp.where(
                    not_last, from_next[at, :].astype(jnp.float32), value - target_ref[at, :].astype(jnp.float32)
                )
                result = (cotangent * slope).astype(jnp.bfloat16)
                pre_grad[at, :] = result
                grad_bias_ref[...] += jnp.sum(result.astype(jnp.float32), axis=0, keepdims=True)
                return carry

            return lax.fori_loop(0, part // 16, step, carry)

        lax.fori_loop(first, first + CHUNKS // 2, piece, 0)
        order = list(range(1, chips)) + [0]
        for j in order:
            input_part(j, 1 - core, part_send, h)
            part_copy(j, h).start()
        for j in order:
            input_part(j, core, own, h)
        for j in range(1, chips):
            part_copy(j, h).wait_recv()
            own[j, side(h), :] = (
                own[j, side(h), :].astype(jnp.float32) + part_recv[j, side(h), :].astype(jnp.float32)
            ).astype(jnp.bfloat16)
            for c in range(first, min(first + CHUNKS // 2, CHUNKS - 1)):
                sum_copy(j, c).start()

    late = sec == sections - 2
    on_time = jnp.logical_not(late)
    backward(0)
    feed(0)
    feed(1)

    @pl.when(on_time)
    def _():
        backward(1)

    def chain(c):
        @pl.when(not_last)
        def _():
            emb_copy(c).wait_recv()

            def add(i, carry):
                at = pl.ds(pl.multiple_of(c * part + i * 16, 16), 16)
                total = emb[at, :] + emb_recv[at, :].astype(jnp.float32)

                @pl.when(not_first)
                def _():
                    emb_send[at, :] = total.astype(jnp.bfloat16)

                @pl.when(sec == 0)
                def _():
                    angular = (
                        fields[at, 0:1] * angle_ref[0:1, :] + fields[at, 1:2] * angle_ref[1:2, :]
                    )
                    feat[me, at, :] = (total + angular).astype(jnp.bfloat16)

                return carry

            lax.fori_loop(0, part // 16, add, 0)

            @pl.when(not_first)
            def _():
                emb_copy(c).start()

            @pl.when(sec == 0)
            def _():
                gather_start(1, feat, c)

    def weight_grad(block):
        def step(t, carry):
            begin = pl.multiple_of(block * width + t * tile, tile)
            column = pl.ds(pl.multiple_of(t * tile, tile), tile)
            grad_w_ref[0, pl.ds(begin, tile), :] = lax.dot_general(
                stash[block, :, column], pre_grad[...], (((0,), (0,)), ((), ())),
                preferred_element_type=jnp.float32,
            ).astype(jnp.bfloat16)
            return carry

        lax.fori_loop(0, width // tile, step, 0)

    blocks = [me, partner]
    for j in range(1, chips):
        blocks += [at_chip(j, core), at_chip(j, 1 - core)]
    @pl.when(on_time)
    def _():
        weight_grad(blocks[0])

    chain(0)
    for c in range(CHUNKS // 2, CHUNKS):
        feed(c)
    for c in range(CHUNKS):
        gather_pass(0, stash, c)
    for c in range(CHUNKS):
        gather_end(0, stash, c)
    for c in range(1, CHUNKS + 1):
        @pl.when(on_time)
        def _():
            for b in blocks[1 + (c - 1) * (shards - 1) // CHUNKS : 1 + c * (shards - 1) // CHUNKS]:
                weight_grad(b)

        if c < CHUNKS:
            chain(c)
            if c == CHUNKS - 1:
                pl.when(on_time)(last_sums)

    @pl.when(late)
    def _():
        backward(1)
        last_sums()

        def every(block, carry):
            weight_grad(block)
            return carry

        lax.fori_loop(0, shards, every, 0)

    def total_grad(c):
        for j in range(1, chips):
            sum_copy(j, c).wait_recv()
        whole = own[0, moving(c), :].astype(jnp.float32) + part_recv[0, moving(c), :].astype(jnp.float32)
        for j in range(1, chips):
            whole = whole + x_recv[j - 1, moving(c), :].astype(jnp.float32)
        grad_in_ref[0, moving(c), :] = whole.astype(jnp.bfloat16)

    def forward(c, carry):
        gather_pass(1, feat, c)

        @pl.when(c > 0)
        def _():
            total_grad(c - 1)

        gather_end(1, feat, c)
        total = jnp.zeros((part, width), jnp.float32)
        for b in range(shards):
            total = total + jnp.dot(
                feat[b, moving(c), :], weight[b * width : (b + 1) * width, :],
                preferred_element_type=jnp.float32,
            )
        fwd_ref[0, moving(c), :] = gelu(total + bias_ref[...]).astype(jnp.bfloat16)
        return carry

    for h in range(2):
        part_copy(0, h).wait_recv()
    lax.fori_loop(0, CHUNKS, forward, 0)
    total_grad(CHUNKS - 1)

    for c in range(CHUNKS):
        gather_drain(0, stash, c)
        gather_drain(1, feat, c)
        for j in range(1, chips):
            sum_copy(j, c).wait_send()
    for h in range(2):
        for j in range(chips):
            part_copy(j, h).wait_send()

    @pl.when(not_last)
    def _():
        for c in range(CHUNKS):
            act_copy(c).wait_send()

    @pl.when(not_first)
    def _():
        for c in range(CHUNKS):
            grad_copy(c).wait_send()
            emb_copy(c).wait_send()


def store(pieces, fwd, grad_in, grad_w, grad_bias, fwd_out, grad_in_out, grad_w_out, grad_bias_out, sem):
    depth = grad_w.shape[1] // pieces
    copies = [(grad_w.at[0, pl.ds(i * depth, depth)], grad_w_out.at[0, pl.ds(i * depth, depth)]) for i in range(pieces)]
    copies += [(fwd, fwd_out), (grad_in, grad_in_out), (grad_bias, grad_bias_out)]
    copies = [pltpu.make_async_copy(src, dst, sem.at[i]) for i, (src, dst) in enumerate(copies)]
    for copy in copies:
        copy.start()
    for copy in copies:
        copy.wait()


def local(sections, shards, *args):
    args = list(args)
    rows, width = args[0].shape[1:]
    table_rows = args[6].shape[0]
    active = args[7].shape[1]
    for k in (7, 8, 9):
        args[k] = args[k].T
    wide = (table_rows + 127) // 128 * 128
    chips = shards // 2
    vmem = pl.BlockSpec(memory_space=pltpu.VMEM)
    hbm = pl.BlockSpec(memory_space=pltpu.HBM)
    smem = pl.BlockSpec(memory_space=pltpu.SMEM)
    dma = pltpu.SemaphoreType.DMA
    half, full = jnp.bfloat16, jnp.float32
    outs = (
        ((1, rows, width), half),
        ((1, rows, width), half),
        ((1, shards * width, width), half),
        ((1, width), full),
    )
    results = pl.pallas_call(
        functools.partial(kernel, sections, shards),
        out_shape=tuple(pltpu.VMEM(*out) for out in outs),
        in_specs=[hbm] * 12 + [smem],
        out_specs=(vmem,) * 4,
        scratch_shapes=[
            pltpu.VMEM((2, rows, width), half),
            pltpu.VMEM((2, rows, width), half),
            pltpu.VMEM((shards * width, width), half),
            pltpu.VMEM((1, width), full),
            pltpu.VMEM((table_rows, width), half),
            pltpu.VMEM((active, rows), jnp.int32),
            pltpu.VMEM((active, rows), full),
            pltpu.VMEM((2, rows), full),
            pltpu.VMEM((2, width), full),
            pltpu.VMEM((rows, width), half),
            pltpu.VMEM((rows, active), jnp.int32),
            pltpu.VMEM((rows, active), full),
            pltpu.VMEM((rows, 8), full),
            pltpu.VMEM((shards, rows, width), half),
            pltpu.VMEM((shards, rows, width), half),
            pltpu.VMEM((rows, width), half),
            pltpu.VMEM((rows, wide), half),
            pltpu.VMEM((rows, width), full),
            pltpu.VMEM((rows, width), half),
            pltpu.VMEM((rows, width), half),
            pltpu.VMEM((rows, width), half),
            pltpu.VMEM((chips, rows, width), half),
            pltpu.VMEM((chips, rows, width), half),
            pltpu.VMEM((chips, rows, width), half),
            pltpu.VMEM((chips - 1, rows, width), half),
            dma((CHUNKS,)),
            dma((9,)),
            dma((3, CHUNKS)),
            dma((3, CHUNKS)),
            dma((2, CHUNKS)),
            dma((2, CHUNKS)),
            dma((2, CHUNKS, chips - 1)),
            dma((2, CHUNKS, chips - 1)),
            dma((2, CHUNKS, chips - 1)),
            dma((2, CHUNKS, chips - 1)),
            dma((chips, 2)),
            dma((chips, 2)),
            dma((chips - 1, CHUNKS)),
            dma((chips - 1, CHUNKS)),
        ],
        compiler_params=pltpu.CompilerParams(
            collective_id=0, has_side_effects=True, vmem_limit_bytes=46 * 1024 * 1024
        ),
        cost_estimate=pl.CostEstimate(
            flops=6 * rows * shards * width * width, bytes_accessed=40 * rows * width, transcendentals=0
        ),
    )(*args)
    any_spec = pl.BlockSpec(memory_space=pl.ANY)
    return pl.pallas_call(
        functools.partial(store, 8),
        out_shape=tuple(jax.ShapeDtypeStruct(*out) for out in outs),
        in_specs=[any_spec] * 4,
        out_specs=(any_spec,) * 4,
        scratch_shapes=[dma((11,))],
        compiler_params=pltpu.CompilerParams(vmem_limit_bytes=1024 * 1024),
    )(*results)


def solution(mesh):
    return jax.shard_map(
        functools.partial(local, mesh.shape["section"], mesh.shape["fsdp"]),
        mesh=mesh,
        in_specs=(
            P("section", "groups", "fsdp"),
            P("section", "groups", "fsdp"),
            P("section", None, "groups", "fsdp"),
            P("section", None, "groups", "fsdp"),
            P("section", None, "fsdp"),
            P("section", "fsdp"),
            P("section", "fsdp"),
            P("groups", None),
            P("groups", None),
            P("groups", None),
            P(None, "fsdp"),
            P("groups", "fsdp"),
            P("section"),
        ),
        out_specs=(
            P("section", "groups", "fsdp"),
            P("section", "groups", "fsdp"),
            P("section", "groups", "fsdp"),
            P("section", ("groups", "fsdp")),
        ),
        check_vma=False,
    )
```

```python
import functools

import jax
import jax.numpy as jnp
from jax import lax
from jax.experimental import pallas as pl
from jax.experimental.pallas import tpu as pltpu
from jax.sharding import PartitionSpec as P

CHUNKS = 4
MESH = pl.DeviceIdType.MESH
ROOT = 0.7978845608028654
CUBIC = 0.044715


def gelu_parts(x):
    squared = x * x
    t = jnp.tanh(ROOT * (x + CUBIC * x * squared))
    half = 0.5 * (1.0 + t)
    slope = half + 0.5 * x * (1.0 - t * t) * (ROOT * (1.0 + 3.0 * CUBIC * squared))
    return x * half, slope


def gelu(x):
    return x * (0.5 * (1.0 + jnp.tanh(ROOT * (x + CUBIC * x * x * x))))


def kernel(
    sections, shards,
    act_hbm, grad_hbm, stash_hbm, pre_hbm, weight_hbm, bias_hbm, table_hbm, index_hbm, amp_hbm,
    field_hbm, angle_hbm, target_hbm, sched_ref,
    fwd_ref, grad_in_ref, grad_w_ref, grad_bias_ref,
    stash_ref, pre_ref, weight, bias_ref, table_ref, index_ref, amp_ref, field_ref, angle_ref, target_ref,
    ids, amps, fields,
    feat, stash, from_next, matrix, emb, emb_recv, emb_send, pre_grad,
    part_send, part_recv, own, x_recv,
    stash_sem, load_sem, z_send, z_recv, near_send, near_recv, far_send, far_recv, pass_send, pass_recv,
    part_send_sem, part_recv_sem, sum_send_sem, sum_recv_sem,
):
    me = lax.axis_index("fsdp")
    sec = lax.axis_index("section")
    chips = shards // 2
    chip, core = me // 2, lax.rem(me, 2)
    partner = chip * 2 + 1 - core
    rows, width = pre_grad.shape
    part = rows // CHUNKS
    tile = min(256, width)

    def at_chip(j, c):
        return lax.rem(chip + j, chips) * 2 + c

    def span(c):
        return pl.ds(c * part, part)

    def moving(c):
        return pl.ds(pl.multiple_of(c * part, part), part)

    def remote(src, dst, send, recv, **where):
        return pltpu.make_async_remote_copy(
            src_ref=src, dst_ref=dst, send_sem=send, recv_sem=recv,
            device_id=where, device_id_type=MESH,
        )

    not_last = sec < sections - 1
    not_first = sec > 0

    pieces = (range(2), range(CHUNKS))

    def piece(g, c):
        if g == 0:
            return pl.ds(0, part) if c == 0 else pl.ds(part, rows - part)
        return moving(c)

    def stash_load(c):
        return pltpu.make_async_copy(stash_hbm.at[0, :, piece(0, c)], stash_ref.at[:, piece(0, c)], stash_sem.at[c])

    loads = {
        name: pltpu.make_async_copy(src, dst, load_sem.at[k])
        for k, (name, src, dst) in enumerate([
            ("index", index_hbm, index_ref),
            ("amp", amp_hbm, amp_ref),
            ("table", table_hbm, table_ref),
            ("pre", pre_hbm.at[0], pre_ref),
            ("target", target_hbm, target_ref),
            ("weight", weight_hbm.at[0], weight),
            ("bias", bias_hbm, bias_ref),
            ("field", field_hbm, field_ref),
            ("angle", angle_hbm, angle_ref),
        ])
    }
    stash_load(0).start()
    barrier = pltpu.get_barrier_semaphore()
    pl.semaphore_signal(barrier, inc=1, device_id={"fsdp": partner}, device_id_type=MESH)
    for j in range(1, chips):
        pl.semaphore_signal(barrier, inc=1, device_id={"fsdp": at_chip(j, core)}, device_id_type=MESH)

    @pl.when(not_last)
    def _():
        pl.semaphore_signal(barrier, inc=1, device_id={"section": sec + 1}, device_id_type=MESH)

    @pl.when(not_first)
    def _():
        pl.semaphore_signal(barrier, inc=1, device_id={"section": sec - 1}, device_id_type=MESH)

    stash_load(1).start()
    for copy in loads.values():
        copy.start()

    def act_copy(c):
        return remote(act_hbm.at[0, moving(c)], feat.at[me, moving(c)], z_send.at[0, c], z_recv.at[0, c], section=sec + 1)

    def grad_copy(c):
        return remote(grad_hbm.at[0, moving(c)], from_next.at[moving(c)], z_send.at[1, c], z_recv.at[1, c], section=sec - 1)

    def emb_copy(c):
        return remote(emb_send.at[moving(c)], emb_recv.at[moving(c)], z_send.at[2, c], z_recv.at[2, c], section=sec - 1)

    def near_copy(g, buf, c, block):
        return remote(buf.at[block, piece(g, c)], buf.at[block, piece(g, c)], near_send.at[g, c], near_recv.at[g, c], fsdp=partner)

    def far_copy(g, buf, c, j, block):
        return remote(buf.at[block, piece(g, c)], buf.at[block, piece(g, c)], far_send.at[g, c, j - 1], far_recv.at[g, c, j - 1], fsdp=at_chip(j, core))

    def pass_copy(g, buf, c, j, block):
        return remote(buf.at[block, piece(g, c)], buf.at[block, piece(g, c)], pass_send.at[g, c, j - 1], pass_recv.at[g, c, j - 1], fsdp=partner)

    def gather_start(g, buf, c):
        for j in range(1, chips):
            far_copy(g, buf, c, j, me).start()
        near_copy(g, buf, c, me).start()

    def gather_pass(g, buf, c):
        for j in range(1, chips):
            block = at_chip(chips - j, core)
            far_copy(g, buf, c, j, block).wait_recv()
            pass_copy(g, buf, c, j, block).start()

    def gather_end(g, buf, c):
        near_copy(g, buf, c, partner).wait_recv()
        for j in range(1, chips):
            pass_copy(g, buf, c, j, at_chip(chips - j, 1 - core)).wait_recv()

    def gather_drain(g, buf, c):
        near_copy(g, buf, c, me).wait_send()
        for j in range(1, chips):
            far_copy(g, buf, c, j, me).wait_send()
            pass_copy(g, buf, c, j, at_chip(chips - j, core)).wait_send()


    slot = sched_ref[0]

    def pick(c):
        at = piece(0, c)
        stash_load(c).wait()
        stash[me, at, :] = jnp.where(slot == 0, stash_ref[0, at, :], stash_ref[1, at, :])

    pick(0)
    pl.semaphore_wait(barrier, chips + jnp.where(not_last, 1, 0) + jnp.where(not_first, 1, 0))
    gather_start(0, stash, 0)

    @pl.when(not_first)
    def _():
        for c in range(CHUNKS // 2):
            grad_copy(c).start()

    @pl.when(not_first & not_last)
    def _():
        grad_copy(CHUNKS // 2).start()

    @pl.when(not_first & (sec < sections - 2))
    def _():
        grad_copy(CHUNKS - 1).start()

    @pl.when(not_last)
    def _():
        for c in range(CHUNKS):
            act_copy(c).start()

    pick(1)
    gather_start(0, stash, 1)

    table_rows = table_ref.shape[0]
    wide = matrix.shape[1]
    base = sec * table_rows

    for name in ("index", "amp", "field", "angle", "table"):
        loads[name].wait()
    ids[...] = index_ref[...].T
    amps[...] = amp_ref[...].T
    fields[...] = jnp.concatenate([field_ref[...], jnp.zeros((6, rows), jnp.float32)], axis=0).T

    def amplitudes(i, carry):
        at = pl.ds(pl.multiple_of(i * 32, 32), 32)
        names = ids[at, :]
        weights = amps[at, :]
        position = lax.broadcasted_iota(jnp.int32, (32, wide), 1) + base
        total = jnp.zeros((32, wide), jnp.float32)
        for k in range(names.shape[1]):
            total = total + jnp.where(names[:, k : k + 1] == position, weights[:, k : k + 1], 0.0)
        matrix[at, :] = total.astype(jnp.bfloat16)
        return carry

    def embed(c, carry):
        lax.fori_loop(c * (part // 32), (c + 1) * (part // 32), amplitudes, 0)
        emb[moving(c), :] = jnp.dot(
            matrix[moving(c), :table_rows], table_ref[...], preferred_element_type=jnp.float32
        )

        @pl.when(jnp.logical_not(not_last))
        def _():
            emb_send[moving(c), :] = emb[moving(c), :].astype(jnp.bfloat16)
            emb_copy(c).start()

        return carry

    lax.fori_loop(0, CHUNKS, embed, 0)

    @pl.when(jnp.logical_not(not_last))
    def _():
        for c in range(CHUNKS // 2, CHUNKS):
            grad_copy(c).start()

    deep = rows // 2

    def side(h):
        return pl.ds(h * deep, deep)

    def input_part(j, c, into, h):
        block = at_chip(j, c)
        for t in range(width // tile):
            begin = pl.multiple_of(block * width + t * tile, tile)
            into[j, side(h), t * tile : (t + 1) * tile] = lax.dot_general(
                pre_grad[side(h), :], weight[pl.ds(begin, tile), :], (((1,), (1,)), ((), ())),
                preferred_element_type=jnp.float32,
            ).astype(jnp.bfloat16)

    def part_copy(j, h):
        return remote(part_send.at[j, side(h)], part_recv.at[j, side(h)], part_send_sem.at[j, h], part_recv_sem.at[j, h], fsdp=partner)

    def sum_rows(c):
        return pl.ds(*((0, deep), (deep, part), (deep + part, part))[c])

    def sum_copy(j, c):
        return remote(own.at[j, sum_rows(c)], x_recv.at[j - 1, sum_rows(c)], sum_send_sem.at[j - 1, c], sum_recv_sem.at[j - 1, c], fsdp=at_chip(j, core))

    for name in ("pre", "target", "weight", "bias"):
        loads[name].wait()
    grad_bias_ref[...] = jnp.zeros_like(grad_bias_ref)

    def feed(c):
        @pl.when(not_first)
        def _():
            act_copy(c).wait_recv()
            gather_start(1, feat, c)

    def send_sums(c):
        for j in range(1, chips):
            sum_copy(j, c).start()

    def backward(h):
        first = h * CHUNKS // 2

        def unit(c, carry):
            @pl.when(not_last)
            def _():
                grad_copy(c).wait_recv()

            def step(i, carry):
                at = pl.ds(pl.multiple_of(c * part + i * 16, 16), 16)
                saved = jnp.where(slot == 0, pre_ref[0, at, :], pre_ref[1, at, :]).astype(jnp.float32)
                value, slope = gelu_parts(saved)
                cotangent = jnp.where(
                    not_last, from_next[at, :].astype(jnp.float32), value - target_ref[at, :].astype(jnp.float32)
                )
                result = (cotangent * slope).astype(jnp.bfloat16)
                pre_grad[at, :] = result
                grad_bias_ref[...] += jnp.sum(result.astype(jnp.float32), axis=0, keepdims=True)
                return carry

            return lax.fori_loop(0, part // 16, step, carry)

        lax.fori_loop(first, first + CHUNKS // 2, unit, 0)
        order = list(range(1, chips)) + [0]
        for j in order:
            input_part(j, 1 - core, part_send, h)
            part_copy(j, h).start()
        for j in order:
            input_part(j, core, own, h)
        for j in range(1, chips):
            part_copy(j, h).wait_recv()
            own[j, side(h), :] = (
                own[j, side(h), :].astype(jnp.float32) + part_recv[j, side(h), :].astype(jnp.float32)
            ).astype(jnp.bfloat16)
            sum_copy(j, h).start()

    late = (sec == sections - 2) | (sec == sections - 3)
    on_time = jnp.logical_not(late)
    backward(0)
    feed(0)
    feed(1)

    def chain(c):
        @pl.when(not_last)
        def _():
            emb_copy(c).wait_recv()

            def add(i, carry):
                at = pl.ds(pl.multiple_of(c * part + i * 16, 16), 16)
                total = emb[at, :] + emb_recv[at, :].astype(jnp.float32)

                @pl.when(not_first)
                def _():
                    emb_send[at, :] = total.astype(jnp.bfloat16)

                @pl.when(sec == 0)
                def _():
                    angular = (
                        fields[at, 0:1] * angle_ref[0:1, :] + fields[at, 1:2] * angle_ref[1:2, :]
                    )
                    feat[me, at, :] = (total + angular).astype(jnp.bfloat16)

                return carry

            lax.fori_loop(0, part // 16, add, 0)

            @pl.when(not_first)
            def _():
                emb_copy(c).start()

            @pl.when(sec == 0)
            def _():
                gather_start(1, feat, c)

    def weight_grad(block):
        def step(t, carry):
            begin = pl.multiple_of(block * width + t * tile, tile)
            column = pl.ds(pl.multiple_of(t * tile, tile), tile)
            grad_w_ref[0, pl.ds(begin, tile), :] = lax.dot_general(
                stash[block, :, column], pre_grad[...], (((0,), (0,)), ((), ())),
                preferred_element_type=jnp.float32,
            ).astype(jnp.bfloat16)
            return carry

        lax.fori_loop(0, width // tile, step, 0)

    blocks = [me, partner]
    for j in range(1, chips):
        blocks += [at_chip(j, core), at_chip(j, 1 - core)]
    def rest():
        for c in range(CHUNKS // 2, CHUNKS):
            feed(c)
        for c in pieces[0]:
            gather_pass(0, stash, c)

    @pl.when(on_time)
    def _():
        backward(1)
        rest()
        weight_grad(blocks[0])

    chain(0)
    pl.when(late)(rest)
    for c in pieces[0]:
        gather_end(0, stash, c)
    for c in range(1, CHUNKS):
        @pl.when(on_time)
        def _():
            for b in blocks[1 + (c - 1) * (shards - 1) // (CHUNKS - 1) : 1 + c * (shards - 1) // (CHUNKS - 1)]:
                weight_grad(b)

        chain(c)

    @pl.when(sec == sections - 2)
    def _():
        grad_copy(CHUNKS - 1).start()

    @pl.when(on_time)
    def _():
        send_sums(2)

    def forward(stop, c, carry):
        @pl.when(c + 1 < stop)
        def _():
            gather_pass(1, feat, c + 1)

        gather_end(1, feat, c)
        total = jnp.zeros((part, width), jnp.float32)
        for b in range(shards):
            total = total + jnp.dot(
                feat[b, moving(c), :], weight[b * width : (b + 1) * width, :],
                preferred_element_type=jnp.float32,
            )
        fwd_ref[0, moving(c), :] = gelu(total + bias_ref[...]).astype(jnp.bfloat16)
        return carry

    early = CHUNKS // 2

    @pl.when(late)
    def _():
        gather_pass(1, feat, 0)
        lax.fori_loop(0, early, functools.partial(forward, early), 0)
        backward(1)
        send_sums(2)

        def every(block, carry):
            weight_grad(block)
            return carry

        lax.fori_loop(0, shards, every, 0)

    def total_grad(c):
        at = sum_rows(c)
        for j in range(1, chips):
            sum_copy(j, c).wait_recv()
        whole = own[0, at, :].astype(jnp.float32) + part_recv[0, at, :].astype(jnp.float32)
        for j in range(1, chips):
            whole = whole + x_recv[j - 1, at, :].astype(jnp.float32)
        grad_in_ref[0, at, :] = whole.astype(jnp.bfloat16)

    for h in range(2):
        part_copy(0, h).wait_recv()
    begin = jnp.where(late, early, 0)
    gather_pass(1, feat, begin)
    lax.fori_loop(begin, CHUNKS, functools.partial(forward, CHUNKS), 0)
    for c in range(3):
        total_grad(c)

    for g, buf in enumerate((stash, feat)):
        for c in pieces[g]:
            gather_drain(g, buf, c)
    for c in range(3):
        for j in range(1, chips):
            sum_copy(j, c).wait_send()
    for h in range(2):
        for j in range(chips):
            part_copy(j, h).wait_send()

    @pl.when(not_last)
    def _():
        for c in range(CHUNKS):
            act_copy(c).wait_send()

    @pl.when(not_first)
    def _():
        for c in range(CHUNKS):
            grad_copy(c).wait_send()
            emb_copy(c).wait_send()


def store(pieces, fwd, grad_in, grad_w, grad_bias, fwd_out, grad_in_out, grad_w_out, grad_bias_out, sem):
    depth = grad_w.shape[1] // pieces
    copies = [(grad_w.at[0, pl.ds(i * depth, depth)], grad_w_out.at[0, pl.ds(i * depth, depth)]) for i in range(pieces)]
    copies += [(fwd, fwd_out), (grad_in, grad_in_out), (grad_bias, grad_bias_out)]
    copies = [pltpu.make_async_copy(src, dst, sem.at[i]) for i, (src, dst) in enumerate(copies)]
    for copy in copies:
        copy.start()
    for copy in copies:
        copy.wait()


def local(sections, shards, *args):
    args = list(args)
    rows, width = args[0].shape[1:]
    table_rows = args[6].shape[0]
    active = args[7].shape[1]
    for k in (7, 8, 9):
        args[k] = args[k].T
    wide = (table_rows + 127) // 128 * 128
    chips = shards // 2
    vmem = pl.BlockSpec(memory_space=pltpu.VMEM)
    hbm = pl.BlockSpec(memory_space=pltpu.HBM)
    dma = pltpu.SemaphoreType.DMA
    half, full = jnp.bfloat16, jnp.float32
    outs = (
        ((1, rows, width), half),
        ((1, rows, width), half),
        ((1, shards * width, width), half),
        ((1, width), full),
    )
    results = pl.pallas_call(
        functools.partial(kernel, sections, shards),
        out_shape=tuple(pltpu.VMEM(*out) for out in outs),
        in_specs=[hbm] * 12 + [pl.BlockSpec(memory_space=pltpu.SMEM)],
        out_specs=(vmem,) * 4,
        scratch_shapes=[
            pltpu.VMEM((2, rows, width), half),
            pltpu.VMEM((2, rows, width), half),
            pltpu.VMEM((shards * width, width), half),
            pltpu.VMEM((1, width), full),
            pltpu.VMEM((table_rows, width), half),
            pltpu.VMEM((active, rows), jnp.int32),
            pltpu.VMEM((active, rows), full),
            pltpu.VMEM((2, rows), full),
            pltpu.VMEM((2, width), full),
            pltpu.VMEM((rows, width), half),
            pltpu.VMEM((rows, active), jnp.int32),
            pltpu.VMEM((rows, active), full),
            pltpu.VMEM((rows, 8), full),
            pltpu.VMEM((shards, rows, width), half),
            pltpu.VMEM((shards, rows, width), half),
            pltpu.VMEM((rows, width), half),
            pltpu.VMEM((rows, wide), half),
            pltpu.VMEM((rows, width), full),
            pltpu.VMEM((rows, width), half),
            pltpu.VMEM((rows, width), half),
            pltpu.VMEM((rows, width), half),
            pltpu.VMEM((chips, rows, width), half),
            pltpu.VMEM((chips, rows, width), half),
            pltpu.VMEM((chips, rows, width), half),
            pltpu.VMEM((chips - 1, rows, width), half),
            dma((2,)),
            dma((9,)),
            dma((3, CHUNKS)),
            dma((3, CHUNKS)),
            dma((2, CHUNKS)),
            dma((2, CHUNKS)),
            dma((2, CHUNKS, chips - 1)),
            dma((2, CHUNKS, chips - 1)),
            dma((2, CHUNKS, chips - 1)),
            dma((2, CHUNKS, chips - 1)),
            dma((chips, 2)),
            dma((chips, 2)),
            dma((chips - 1, 3)),
            dma((chips - 1, 3)),
        ],
        compiler_params=pltpu.CompilerParams(
            collective_id=0, has_side_effects=True, vmem_limit_bytes=46 * 1024 * 1024
        ),
        cost_estimate=pl.CostEstimate(
            flops=6 * rows * shards * width * width, bytes_accessed=40 * rows * width, transcendentals=0
        ),
    )(*args)
    any_spec = pl.BlockSpec(memory_space=pl.ANY)
    return pl.pallas_call(
        functools.partial(store, 8),
        out_shape=tuple(jax.ShapeDtypeStruct(*out) for out in outs),
        in_specs=[any_spec] * 4,
        out_specs=(any_spec,) * 4,
        scratch_shapes=[dma((11,))],
        compiler_params=pltpu.CompilerParams(vmem_limit_bytes=1024 * 1024),
    )(*results)


def solution(mesh):
    return jax.shard_map(
        functools.partial(local, mesh.shape["section"], mesh.shape["fsdp"]),
        mesh=mesh,
        in_specs=(
            P("section", "groups", "fsdp"),
            P("section", "groups", "fsdp"),
            P("section", None, "groups", "fsdp"),
            P("section", None, "groups", "fsdp"),
            P("section", None, "fsdp"),
            P("section", "fsdp"),
            P("section", "fsdp"),
            P("groups", None),
            P("groups", None),
            P("groups", None),
            P(None, "fsdp"),
            P("groups", "fsdp"),
            P("section"),
        ),
        out_specs=(
            P("section", "groups", "fsdp"),
            P("section", "groups", "fsdp"),
            P("section", "groups", "fsdp"),
            P("section", ("groups", "fsdp")),
        ),
        check_vma=False,
    )
```

```python
import functools

import jax
import jax.numpy as jnp
from jax import lax
from jax.experimental import pallas as pl
from jax.experimental.pallas import tpu as pltpu
from jax.sharding import PartitionSpec as P

CHUNKS = 4
LAST = 32
MESH = pl.DeviceIdType.MESH
ROOT = 0.7978845608028654
CUBIC = 0.044715


def gelu_parts(x):
    squared = x * x
    t = jnp.tanh(ROOT * (x + CUBIC * x * squared))
    half = 0.5 * (1.0 + t)
    slope = half + 0.5 * x * (1.0 - t * t) * (ROOT * (1.0 + 3.0 * CUBIC * squared))
    return x * half, slope


def gelu(x):
    return x * (0.5 * (1.0 + jnp.tanh(ROOT * (x + CUBIC * x * x * x))))


def kernel(
    sections, shards,
    act_hbm, grad_hbm, stash_hbm, pre_hbm, weight_hbm, bias_hbm, table_hbm, index_hbm, amp_hbm,
    field_hbm, angle_hbm, target_hbm, sched_ref,
    fwd_ref, grad_in_ref, grad_w_ref, grad_bias_ref,
    stash_ref, pre_ref, weight, bias_ref, table_ref, index_ref, amp_ref, field_ref, angle_ref, target_ref,
    ids, amps, fields,
    feat, stash, from_next, matrix, emb, emb_recv, emb_send, pre_grad,
    part_send, part_recv, own, x_recv,
    stash_sem, load_sem, z_send, z_recv, near_send, near_recv, far_send, far_recv, pass_send, pass_recv,
    part_send_sem, part_recv_sem, sum_send_sem, sum_recv_sem,
):
    me = lax.axis_index("fsdp")
    sec = lax.axis_index("section")
    chips = shards // 2
    chip, core = me // 2, lax.rem(me, 2)
    partner = chip * 2 + 1 - core
    rows, width = pre_grad.shape
    part = rows // CHUNKS
    tile = min(256, width)

    def at_chip(j, c):
        return lax.rem(chip + j, chips) * 2 + c

    def span(c):
        return pl.ds(c * part, part)

    def moving(c):
        return pl.ds(pl.multiple_of(c * part, part), part)

    def remote(src, dst, send, recv, **where):
        return pltpu.make_async_remote_copy(
            src_ref=src, dst_ref=dst, send_sem=send, recv_sem=recv,
            device_id=where, device_id_type=MESH,
        )

    not_last = sec < sections - 1
    not_first = sec > 0

    pieces = (range(2), range(CHUNKS))

    def piece(g, c):
        if g == 0:
            return pl.ds(0, part) if c == 0 else pl.ds(part, rows - part)
        return moving(c)

    def stash_load(c):
        return pltpu.make_async_copy(stash_hbm.at[0, :, piece(0, c)], stash_ref.at[:, piece(0, c)], stash_sem.at[c])

    loads = {
        name: pltpu.make_async_copy(src, dst, load_sem.at[k])
        for k, (name, src, dst) in enumerate([
            ("index", index_hbm, index_ref),
            ("amp", amp_hbm, amp_ref),
            ("table", table_hbm, table_ref),
            ("pre", pre_hbm.at[0], pre_ref),
            ("target", target_hbm, target_ref),
            ("weight", weight_hbm.at[0], weight),
            ("bias", bias_hbm, bias_ref),
            ("field", field_hbm, field_ref),
            ("angle", angle_hbm, angle_ref),
        ])
    }
    stash_load(0).start()
    barrier = pltpu.get_barrier_semaphore()
    pl.semaphore_signal(barrier, inc=1, device_id={"fsdp": partner}, device_id_type=MESH)
    for j in range(1, chips):
        pl.semaphore_signal(barrier, inc=1, device_id={"fsdp": at_chip(j, core)}, device_id_type=MESH)

    @pl.when(not_last)
    def _():
        pl.semaphore_signal(barrier, inc=1, device_id={"section": sec + 1}, device_id_type=MESH)

    @pl.when(not_first)
    def _():
        pl.semaphore_signal(barrier, inc=1, device_id={"section": sec - 1}, device_id_type=MESH)

    stash_load(1).start()
    for copy in loads.values():
        copy.start()

    def act_copy(c):
        return remote(act_hbm.at[0, moving(c)], feat.at[me, moving(c)], z_send.at[0, c], z_recv.at[0, c], section=sec + 1)

    def grad_copy(c):
        return remote(grad_hbm.at[0, moving(c)], from_next.at[moving(c)], z_send.at[1, c], z_recv.at[1, c], section=sec - 1)

    def emb_copy(c):
        return remote(emb_send.at[moving(c)], emb_recv.at[moving(c)], z_send.at[2, c], z_recv.at[2, c], section=sec - 1)

    def near_copy(g, buf, c, block):
        return remote(buf.at[block, piece(g, c)], buf.at[block, piece(g, c)], near_send.at[g, c], near_recv.at[g, c], fsdp=partner)

    def far_copy(g, buf, c, j, block):
        return remote(buf.at[block, piece(g, c)], buf.at[block, piece(g, c)], far_send.at[g, c, j - 1], far_recv.at[g, c, j - 1], fsdp=at_chip(j, core))

    def pass_copy(g, buf, c, j, block):
        return remote(buf.at[block, piece(g, c)], buf.at[block, piece(g, c)], pass_send.at[g, c, j - 1], pass_recv.at[g, c, j - 1], fsdp=partner)

    def gather_start(g, buf, c):
        for j in range(1, chips):
            far_copy(g, buf, c, j, me).start()
        near_copy(g, buf, c, me).start()

    def gather_pass(g, buf, c):
        for j in range(1, chips):
            block = at_chip(chips - j, core)
            far_copy(g, buf, c, j, block).wait_recv()
            pass_copy(g, buf, c, j, block).start()

    def gather_end(g, buf, c):
        near_copy(g, buf, c, partner).wait_recv()
        for j in range(1, chips):
            pass_copy(g, buf, c, j, at_chip(chips - j, 1 - core)).wait_recv()

    def gather_drain(g, buf, c):
        near_copy(g, buf, c, me).wait_send()
        for j in range(1, chips):
            far_copy(g, buf, c, j, me).wait_send()
            pass_copy(g, buf, c, j, at_chip(chips - j, core)).wait_send()


    slot = sched_ref[0]

    def pick(c):
        at = piece(0, c)
        stash_load(c).wait()
        stash[me, at, :] = jnp.where(slot == 0, stash_ref[0, at, :], stash_ref[1, at, :])

    pick(0)
    pl.semaphore_wait(barrier, chips + jnp.where(not_last, 1, 0) + jnp.where(not_first, 1, 0))
    gather_start(0, stash, 0)

    @pl.when(not_first)
    def _():
        for c in range(CHUNKS // 2):
            grad_copy(c).start()

    @pl.when(not_first & not_last)
    def _():
        grad_copy(CHUNKS // 2).start()

    @pl.when(not_first & (sec < sections - 2))
    def _():
        grad_copy(CHUNKS - 1).start()

    @pl.when(not_last)
    def _():
        for c in range(CHUNKS):
            act_copy(c).start()

    pick(1)
    gather_start(0, stash, 1)

    table_rows = table_ref.shape[0]
    wide = matrix.shape[1]
    base = sec * table_rows

    for name in ("index", "amp", "field", "angle", "table"):
        loads[name].wait()
    ids[...] = index_ref[...].T
    amps[...] = amp_ref[...].T
    fields[...] = jnp.concatenate([field_ref[...], jnp.zeros((6, rows), jnp.float32)], axis=0).T

    def amplitudes(i, carry):
        at = pl.ds(pl.multiple_of(i * 32, 32), 32)
        names = ids[at, :]
        weights = amps[at, :]
        position = lax.broadcasted_iota(jnp.int32, (32, wide), 1) + base
        total = jnp.zeros((32, wide), jnp.float32)
        for k in range(names.shape[1]):
            total = total + jnp.where(names[:, k : k + 1] == position, weights[:, k : k + 1], 0.0)
        matrix[at, :] = total.astype(jnp.bfloat16)
        return carry

    def embed(c, carry):
        lax.fori_loop(c * (part // 32), (c + 1) * (part // 32), amplitudes, 0)
        emb[moving(c), :] = jnp.dot(
            matrix[moving(c), :table_rows], table_ref[...], preferred_element_type=jnp.float32
        )

        @pl.when(jnp.logical_not(not_last))
        def _():
            emb_send[moving(c), :] = emb[moving(c), :].astype(jnp.bfloat16)
            emb_copy(c).start()

        return carry

    lax.fori_loop(0, CHUNKS, embed, 0)

    @pl.when(jnp.logical_not(not_last))
    def _():
        for c in range(CHUNKS // 2, CHUNKS):
            grad_copy(c).start()

    deep = rows // 2

    def side(h):
        return pl.ds(h * deep, deep)

    def input_part(j, c, into, h):
        block = at_chip(j, c)
        for t in range(width // tile):
            begin = pl.multiple_of(block * width + t * tile, tile)
            into[j, side(h), t * tile : (t + 1) * tile] = lax.dot_general(
                pre_grad[side(h), :], weight[pl.ds(begin, tile), :], (((1,), (1,)), ((), ())),
                preferred_element_type=jnp.float32,
            ).astype(jnp.bfloat16)

    def part_copy(j, h):
        return remote(part_send.at[j, side(h)], part_recv.at[j, side(h)], part_send_sem.at[j, h], part_recv_sem.at[j, h], fsdp=partner)

    def sum_rows(c):
        return pl.ds(*((0, deep), (deep, part), (deep + part, part - LAST), (rows - LAST, LAST))[c])

    def sum_copy(j, c):
        return remote(own.at[j, sum_rows(c)], x_recv.at[j - 1, sum_rows(c)], sum_send_sem.at[j - 1, c], sum_recv_sem.at[j - 1, c], fsdp=at_chip(j, core))

    for name in ("pre", "target", "weight", "bias"):
        loads[name].wait()
    grad_bias_ref[...] = jnp.zeros_like(grad_bias_ref)

    def feed(c):
        @pl.when(not_first)
        def _():
            act_copy(c).wait_recv()
            gather_start(1, feat, c)

    def send_sums(c):
        for j in range(1, chips):
            sum_copy(j, c).start()

    def backward(h):
        first = h * CHUNKS // 2

        def unit(c, carry):
            @pl.when(not_last)
            def _():
                grad_copy(c).wait_recv()

            def step(i, carry):
                at = pl.ds(pl.multiple_of(c * part + i * 16, 16), 16)
                saved = jnp.where(slot == 0, pre_ref[0, at, :], pre_ref[1, at, :]).astype(jnp.float32)
                value, slope = gelu_parts(saved)
                cotangent = jnp.where(
                    not_last, from_next[at, :].astype(jnp.float32), value - target_ref[at, :].astype(jnp.float32)
                )
                result = (cotangent * slope).astype(jnp.bfloat16)
                pre_grad[at, :] = result
                grad_bias_ref[...] += jnp.sum(result.astype(jnp.float32), axis=0, keepdims=True)
                return carry

            return lax.fori_loop(0, part // 16, step, carry)

        lax.fori_loop(first, first + CHUNKS // 2, unit, 0)
        order = list(range(1, chips)) + [0]
        for j in order:
            input_part(j, 1 - core, part_send, h)
            part_copy(j, h).start()
        for j in order:
            input_part(j, core, own, h)
        for j in range(1, chips):
            part_copy(j, h).wait_recv()
            own[j, side(h), :] = (
                own[j, side(h), :].astype(jnp.float32) + part_recv[j, side(h), :].astype(jnp.float32)
            ).astype(jnp.bfloat16)
            sum_copy(j, h).start()

    late = (sec == sections - 2) | (sec == sections - 3)
    on_time = jnp.logical_not(late)
    backward(0)
    feed(0)
    feed(1)

    def chain(c):
        @pl.when(not_last)
        def _():
            emb_copy(c).wait_recv()

            def add(i, carry):
                at = pl.ds(pl.multiple_of(c * part + i * 16, 16), 16)
                total = emb[at, :] + emb_recv[at, :].astype(jnp.float32)

                @pl.when(not_first)
                def _():
                    emb_send[at, :] = total.astype(jnp.bfloat16)

                @pl.when(sec == 0)
                def _():
                    angular = (
                        fields[at, 0:1] * angle_ref[0:1, :] + fields[at, 1:2] * angle_ref[1:2, :]
                    )
                    feat[me, at, :] = (total + angular).astype(jnp.bfloat16)

                return carry

            lax.fori_loop(0, part // 16, add, 0)

            @pl.when(not_first)
            def _():
                emb_copy(c).start()

            @pl.when(sec == 0)
            def _():
                gather_start(1, feat, c)

    def weight_grad(block):
        def step(t, carry):
            begin = pl.multiple_of(block * width + t * tile, tile)
            column = pl.ds(pl.multiple_of(t * tile, tile), tile)
            grad_w_ref[0, pl.ds(begin, tile), :] = lax.dot_general(
                stash[block, :, column], pre_grad[...], (((0,), (0,)), ((), ())),
                preferred_element_type=jnp.float32,
            ).astype(jnp.bfloat16)
            return carry

        lax.fori_loop(0, width // tile, step, 0)

    blocks = [me, partner]
    for j in range(1, chips):
        blocks += [at_chip(j, core), at_chip(j, 1 - core)]
    def rest():
        for c in range(CHUNKS // 2, CHUNKS):
            feed(c)
        for c in pieces[0]:
            gather_pass(0, stash, c)

    @pl.when(on_time)
    def _():
        backward(1)
        rest()
        weight_grad(blocks[0])

    chain(0)
    pl.when(late)(rest)
    for c in pieces[0]:
        gather_end(0, stash, c)
    for c in range(1, CHUNKS):
        @pl.when(on_time)
        def _():
            for b in blocks[1 + (c - 1) * (shards - 1) // (CHUNKS - 1) : 1 + c * (shards - 1) // (CHUNKS - 1)]:
                weight_grad(b)

        chain(c)

    @pl.when(sec == sections - 2)
    def _():
        grad_copy(CHUNKS - 1).start()

    @pl.when(on_time)
    def _():
        send_sums(2)
        send_sums(3)

    def forward(stop, c, carry):
        @pl.when(c + 1 < stop)
        def _():
            gather_pass(1, feat, c + 1)

        gather_end(1, feat, c)
        total = jnp.zeros((part, width), jnp.float32)
        for b in range(shards):
            total = total + jnp.dot(
                feat[b, moving(c), :], weight[b * width : (b + 1) * width, :],
                preferred_element_type=jnp.float32,
            )
        fwd_ref[0, moving(c), :] = gelu(total + bias_ref[...]).astype(jnp.bfloat16)
        return carry

    early = CHUNKS // 2

    @pl.when(late)
    def _():
        gather_pass(1, feat, 0)
        lax.fori_loop(0, early, functools.partial(forward, early), 0)
        backward(1)
        send_sums(2)
        send_sums(3)

        def every(block, carry):
            weight_grad(block)
            return carry

        lax.fori_loop(0, shards, every, 0)

    def total_grad(c):
        at = sum_rows(c)
        for j in range(1, chips):
            sum_copy(j, c).wait_recv()
        whole = own[0, at, :].astype(jnp.float32) + part_recv[0, at, :].astype(jnp.float32)
        for j in range(1, chips):
            whole = whole + x_recv[j - 1, at, :].astype(jnp.float32)
        grad_in_ref[0, at, :] = whole.astype(jnp.bfloat16)

    for h in range(2):
        part_copy(0, h).wait_recv()
    begin = jnp.where(late, early, 0)
    gather_pass(1, feat, begin)
    lax.fori_loop(begin, CHUNKS, functools.partial(forward, CHUNKS), 0)
    for c in range(3):
        total_grad(c)

    for g, buf in enumerate((stash, feat)):
        for c in pieces[g]:
            gather_drain(g, buf, c)
    for h in range(2):
        for j in range(chips):
            part_copy(j, h).wait_send()

    @pl.when(not_last)
    def _():
        for c in range(CHUNKS):
            act_copy(c).wait_send()

    @pl.when(not_first)
    def _():
        for c in range(CHUNKS):
            grad_copy(c).wait_send()
            emb_copy(c).wait_send()

    total_grad(3)
    for c in range(4):
        for j in range(1, chips):
            sum_copy(j, c).wait_send()


def store(pieces, fwd, grad_in, grad_w, grad_bias, fwd_out, grad_in_out, grad_w_out, grad_bias_out, sem):
    depth = grad_w.shape[1] // pieces
    copies = [(grad_w.at[0, pl.ds(i * depth, depth)], grad_w_out.at[0, pl.ds(i * depth, depth)]) for i in range(pieces)]
    copies += [(fwd, fwd_out), (grad_in, grad_in_out), (grad_bias, grad_bias_out)]
    copies = [pltpu.make_async_copy(src, dst, sem.at[i]) for i, (src, dst) in enumerate(copies)]
    for copy in copies:
        copy.start()
    for copy in copies:
        copy.wait()


def local(sections, shards, *args):
    args = list(args)
    rows, width = args[0].shape[1:]
    table_rows = args[6].shape[0]
    active = args[7].shape[1]
    for k in (7, 8, 9):
        args[k] = args[k].T
    wide = (table_rows + 127) // 128 * 128
    chips = shards // 2
    vmem = pl.BlockSpec(memory_space=pltpu.VMEM)
    hbm = pl.BlockSpec(memory_space=pltpu.HBM)
    dma = pltpu.SemaphoreType.DMA
    half, full = jnp.bfloat16, jnp.float32
    outs = (
        ((1, rows, width), half),
        ((1, rows, width), half),
        ((1, shards * width, width), half),
        ((1, width), full),
    )
    results = pl.pallas_call(
        functools.partial(kernel, sections, shards),
        out_shape=tuple(pltpu.VMEM(*out) for out in outs),
        in_specs=[hbm] * 12 + [pl.BlockSpec(memory_space=pltpu.SMEM)],
        out_specs=(vmem,) * 4,
        scratch_shapes=[
            pltpu.VMEM((2, rows, width), half),
            pltpu.VMEM((2, rows, width), half),
            pltpu.VMEM((shards * width, width), half),
            pltpu.VMEM((1, width), full),
            pltpu.VMEM((table_rows, width), half),
            pltpu.VMEM((active, rows), jnp.int32),
            pltpu.VMEM((active, rows), full),
            pltpu.VMEM((2, rows), full),
            pltpu.VMEM((2, width), full),
            pltpu.VMEM((rows, width), half),
            pltpu.VMEM((rows, active), jnp.int32),
            pltpu.VMEM((rows, active), full),
            pltpu.VMEM((rows, 8), full),
            pltpu.VMEM((shards, rows, width), half),
            pltpu.VMEM((shards, rows, width), half),
            pltpu.VMEM((rows, width), half),
            pltpu.VMEM((rows, wide), half),
            pltpu.VMEM((rows, width), full),
            pltpu.VMEM((rows, width), half),
            pltpu.VMEM((rows, width), half),
            pltpu.VMEM((rows, width), half),
            pltpu.VMEM((chips, rows, width), half),
            pltpu.VMEM((chips, rows, width), half),
            pltpu.VMEM((chips, rows, width), half),
            pltpu.VMEM((chips - 1, rows, width), half),
            dma((2,)),
            dma((9,)),
            dma((3, CHUNKS)),
            dma((3, CHUNKS)),
            dma((2, CHUNKS)),
            dma((2, CHUNKS)),
            dma((2, CHUNKS, chips - 1)),
            dma((2, CHUNKS, chips - 1)),
            dma((2, CHUNKS, chips - 1)),
            dma((2, CHUNKS, chips - 1)),
            dma((chips, 2)),
            dma((chips, 2)),
            dma((chips - 1, 4)),
            dma((chips - 1, 4)),
        ],
        compiler_params=pltpu.CompilerParams(
            collective_id=0, has_side_effects=True, vmem_limit_bytes=46 * 1024 * 1024
        ),
        cost_estimate=pl.CostEstimate(
            flops=6 * rows * shards * width * width, bytes_accessed=40 * rows * width, transcendentals=0
        ),
    )(*args)
    any_spec = pl.BlockSpec(memory_space=pl.ANY)
    return pl.pallas_call(
        functools.partial(store, 8),
        out_shape=tuple(jax.ShapeDtypeStruct(*out) for out in outs),
        in_specs=[any_spec] * 4,
        out_specs=(any_spec,) * 4,
        scratch_shapes=[dma((11,))],
        compiler_params=pltpu.CompilerParams(vmem_limit_bytes=1024 * 1024),
    )(*results)


def solution(mesh):
    return jax.shard_map(
        functools.partial(local, mesh.shape["section"], mesh.shape["fsdp"]),
        mesh=mesh,
        in_specs=(
            P("section", "groups", "fsdp"),
            P("section", "groups", "fsdp"),
            P("section", None, "groups", "fsdp"),
            P("section", None, "groups", "fsdp"),
            P("section", None, "fsdp"),
            P("section", "fsdp"),
            P("section", "fsdp"),
            P("groups", None),
            P("groups", None),
            P("groups", None),
            P(None, "fsdp"),
            P("groups", "fsdp"),
            P("section"),
        ),
        out_specs=(
            P("section", "groups", "fsdp"),
            P("section", "groups", "fsdp"),
            P("section", "groups", "fsdp"),
            P("section", ("groups", "fsdp")),
        ),
        check_vma=False,
    )
```

```python
import functools

import jax
import jax.numpy as jnp
from jax import lax
from jax.experimental import pallas as pl
from jax.experimental.pallas import tpu as pltpu
from jax.sharding import PartitionSpec as P

CHUNKS = 4
LAST = 32
MESH = pl.DeviceIdType.MESH
ROOT = 0.7978845608028654
CUBIC = 0.044715


def gelu_parts(x):
    squared = x * x
    t = jnp.tanh(ROOT * (x + CUBIC * x * squared))
    half = 0.5 * (1.0 + t)
    slope = half + 0.5 * x * (1.0 - t * t) * (ROOT * (1.0 + 3.0 * CUBIC * squared))
    return x * half, slope


def gelu(x):
    return x * (0.5 * (1.0 + jnp.tanh(ROOT * (x + CUBIC * x * x * x))))


def kernel(
    sections, shards,
    act_hbm, grad_hbm, stash_hbm, pre_hbm, weight_hbm, bias_hbm, table_hbm, index_hbm, amp_hbm,
    field_hbm, angle_hbm, target_hbm, sched_ref,
    fwd_ref, grad_in_ref, grad_w_ref, grad_bias_ref,
    stash_ref, pre_ref, weight, bias_ref, table_ref, index_ref, amp_ref, field_ref, angle_ref, target_ref,
    ids, amps, fields,
    feat, stash, from_next, matrix, emb, emb_recv, emb_send, pre_grad,
    part_send, part_recv, own, x_recv,
    stash_sem, load_sem, z_send, z_recv, near_send, near_recv, far_send, far_recv, pass_send, pass_recv,
    part_send_sem, part_recv_sem, sum_send_sem, sum_recv_sem,
):
    me = lax.axis_index("fsdp")
    sec = lax.axis_index("section")
    chips = shards // 2
    chip, core = me // 2, lax.rem(me, 2)
    partner = chip * 2 + 1 - core
    rows, width = pre_grad.shape
    part = rows // CHUNKS
    tile = min(256, width)

    def at_chip(j, c):
        return lax.rem(chip + j, chips) * 2 + c

    def span(c):
        return pl.ds(c * part, part)

    def moving(c):
        return pl.ds(pl.multiple_of(c * part, part), part)

    def remote(src, dst, send, recv, **where):
        return pltpu.make_async_remote_copy(
            src_ref=src, dst_ref=dst, send_sem=send, recv_sem=recv,
            device_id=where, device_id_type=MESH,
        )

    not_last = sec < sections - 1
    not_first = sec > 0

    pieces = (range(2), range(CHUNKS))

    def piece(g, c):
        if g == 0:
            return pl.ds(0, 2 * part) if c == 0 else pl.ds(2 * part, rows - 2 * part)
        return moving(c)

    def stash_load(c):
        return pltpu.make_async_copy(stash_hbm.at[0, :, piece(0, c)], stash_ref.at[:, piece(0, c)], stash_sem.at[c])

    loads = {
        name: pltpu.make_async_copy(src, dst, load_sem.at[k])
        for k, (name, src, dst) in enumerate([
            ("index", index_hbm, index_ref),
            ("amp", amp_hbm, amp_ref),
            ("table", table_hbm, table_ref),
            ("pre", pre_hbm.at[0], pre_ref),
            ("target", target_hbm, target_ref),
            ("weight", weight_hbm.at[0], weight),
            ("bias", bias_hbm, bias_ref),
            ("field", field_hbm, field_ref),
            ("angle", angle_hbm, angle_ref),
        ])
    }
    barrier = pltpu.get_barrier_semaphore()
    pl.semaphore_signal(barrier, inc=1, device_id={"fsdp": partner}, device_id_type=MESH)
    for j in range(1, chips):
        pl.semaphore_signal(barrier, inc=1, device_id={"fsdp": at_chip(j, core)}, device_id_type=MESH)

    stash_load(0).start()

    @pl.when(not_last)
    def _():
        pl.semaphore_signal(barrier, inc=1, device_id={"section": sec + 1}, device_id_type=MESH)

    @pl.when(not_first)
    def _():
        pl.semaphore_signal(barrier, inc=1, device_id={"section": sec - 1}, device_id_type=MESH)

    stash_load(1).start()
    for copy in loads.values():
        copy.start()

    def act_copy(c):
        return remote(act_hbm.at[0, moving(c)], feat.at[me, moving(c)], z_send.at[0, c], z_recv.at[0, c], section=sec + 1)

    def grad_copy(c):
        return remote(grad_hbm.at[0, moving(c)], from_next.at[moving(c)], z_send.at[1, c], z_recv.at[1, c], section=sec - 1)

    def emb_copy(c):
        return remote(emb_send.at[moving(c)], emb_recv.at[moving(c)], z_send.at[2, c], z_recv.at[2, c], section=sec - 1)

    def near_copy(g, buf, c, block):
        return remote(buf.at[block, piece(g, c)], buf.at[block, piece(g, c)], near_send.at[g, c], near_recv.at[g, c], fsdp=partner)

    def far_copy(g, buf, c, j, block):
        return remote(buf.at[block, piece(g, c)], buf.at[block, piece(g, c)], far_send.at[g, c, j - 1], far_recv.at[g, c, j - 1], fsdp=at_chip(j, core))

    def pass_copy(g, buf, c, j, block):
        return remote(buf.at[block, piece(g, c)], buf.at[block, piece(g, c)], pass_send.at[g, c, j - 1], pass_recv.at[g, c, j - 1], fsdp=partner)

    def gather_start(g, buf, c):
        for j in range(1, chips):
            far_copy(g, buf, c, j, me).start()
        near_copy(g, buf, c, me).start()

    def gather_pass(g, buf, c):
        for j in range(1, chips):
            block = at_chip(chips - j, core)
            far_copy(g, buf, c, j, block).wait_recv()
            pass_copy(g, buf, c, j, block).start()

    def gather_end(g, buf, c):
        near_copy(g, buf, c, partner).wait_recv()
        for j in range(1, chips):
            pass_copy(g, buf, c, j, at_chip(chips - j, 1 - core)).wait_recv()

    def gather_drain(g, buf, c):
        near_copy(g, buf, c, me).wait_send()
        for j in range(1, chips):
            far_copy(g, buf, c, j, me).wait_send()
            pass_copy(g, buf, c, j, at_chip(chips - j, core)).wait_send()


    slot = sched_ref[0]

    def pick(c):
        at = piece(0, c)
        stash_load(c).wait()
        stash[me, at, :] = jnp.where(slot == 0, stash_ref[0, at, :], stash_ref[1, at, :])

    pick(0)
    pl.semaphore_wait(barrier, chips + jnp.where(not_last, 1, 0) + jnp.where(not_first, 1, 0))
    gather_start(0, stash, 0)

    @pl.when(not_first)
    def _():
        for c in range(CHUNKS // 2):
            grad_copy(c).start()

    @pl.when(not_first & not_last)
    def _():
        grad_copy(CHUNKS // 2).start()

    @pl.when(not_first & (sec < sections - 2))
    def _():
        grad_copy(CHUNKS - 1).start()

    @pl.when(not_last)
    def _():
        for c in range(CHUNKS):
            act_copy(c).start()

    pick(1)
    gather_start(0, stash, 1)

    table_rows = table_ref.shape[0]
    wide = matrix.shape[1]
    base = sec * table_rows

    for name in ("index", "amp", "field", "angle", "table"):
        loads[name].wait()
    ids[...] = index_ref[...].T
    amps[...] = amp_ref[...].T
    fields[...] = jnp.concatenate([field_ref[...], jnp.zeros((6, rows), jnp.float32)], axis=0).T

    def amplitudes(i, carry):
        at = pl.ds(pl.multiple_of(i * 32, 32), 32)
        names = ids[at, :]
        weights = amps[at, :]
        position = lax.broadcasted_iota(jnp.int32, (32, wide), 1) + base
        total = jnp.zeros((32, wide), jnp.float32)
        for k in range(names.shape[1]):
            total = total + jnp.where(names[:, k : k + 1] == position, weights[:, k : k + 1], 0.0)
        matrix[at, :] = total.astype(jnp.bfloat16)
        return carry

    def embed(c, carry):
        lax.fori_loop(c * (part // 32), (c + 1) * (part // 32), amplitudes, 0)
        emb[moving(c), :] = jnp.dot(
            matrix[moving(c), :table_rows], table_ref[...], preferred_element_type=jnp.float32
        )

        @pl.when(jnp.logical_not(not_last))
        def _():
            emb_send[moving(c), :] = emb[moving(c), :].astype(jnp.bfloat16)
            emb_copy(c).start()

        return carry

    lax.fori_loop(0, CHUNKS, embed, 0)

    @pl.when(jnp.logical_not(not_last))
    def _():
        for c in range(CHUNKS // 2, CHUNKS):
            grad_copy(c).start()

    deep = rows // 2

    def side(h):
        return pl.ds(h * deep, deep)

    def input_part(j, c, into, h):
        block = at_chip(j, c)
        for t in range(width // tile):
            begin = pl.multiple_of(block * width + t * tile, tile)
            into[j, side(h), t * tile : (t + 1) * tile] = lax.dot_general(
                pre_grad[side(h), :], weight[pl.ds(begin, tile), :], (((1,), (1,)), ((), ())),
                preferred_element_type=jnp.float32,
            ).astype(jnp.bfloat16)

    def part_copy(j, h):
        return remote(part_send.at[j, side(h)], part_recv.at[j, side(h)], part_send_sem.at[j, h], part_recv_sem.at[j, h], fsdp=partner)

    def sum_rows(c):
        return pl.ds(*((0, deep), (deep, part), (deep + part, part - LAST), (rows - LAST, LAST))[c])

    def sum_copy(j, c):
        return remote(own.at[j, sum_rows(c)], x_recv.at[j - 1, sum_rows(c)], sum_send_sem.at[j - 1, c], sum_recv_sem.at[j - 1, c], fsdp=at_chip(j, core))

    for name in ("pre", "target", "weight", "bias"):
        loads[name].wait()
    grad_bias_ref[...] = jnp.zeros_like(grad_bias_ref)

    def feed(c):
        @pl.when(not_first)
        def _():
            act_copy(c).wait_recv()
            gather_start(1, feat, c)

    def send_sums(c):
        for j in range(1, chips):
            sum_copy(j, c).start()

    def backward(h):
        first = h * CHUNKS // 2

        def unit(c, carry):
            @pl.when(not_last)
            def _():
                grad_copy(c).wait_recv()

            def step(i, carry):
                at = pl.ds(pl.multiple_of(c * part + i * 16, 16), 16)
                saved = jnp.where(slot == 0, pre_ref[0, at, :], pre_ref[1, at, :]).astype(jnp.float32)
                value, slope = gelu_parts(saved)
                cotangent = jnp.where(
                    not_last, from_next[at, :].astype(jnp.float32), value - target_ref[at, :].astype(jnp.float32)
                )
                result = (cotangent * slope).astype(jnp.bfloat16)
                pre_grad[at, :] = result
                grad_bias_ref[...] += jnp.sum(result.astype(jnp.float32), axis=0, keepdims=True)
                return carry

            return lax.fori_loop(0, part // 16, step, carry)

        lax.fori_loop(first, first + CHUNKS // 2, unit, 0)
        order = list(range(1, chips)) + [0]
        for j in order:
            input_part(j, 1 - core, part_send, h)
            part_copy(j, h).start()
        for j in order:
            input_part(j, core, own, h)
        for j in range(1, chips):
            part_copy(j, h).wait_recv()
            own[j, side(h), :] = (
                own[j, side(h), :].astype(jnp.float32) + part_recv[j, side(h), :].astype(jnp.float32)
            ).astype(jnp.bfloat16)
            sum_copy(j, h).start()

    late = (sec == sections - 2) | (sec == sections - 3)
    on_time = jnp.logical_not(late)
    backward(0)
    feed(0)
    feed(1)

    def chain(c):
        @pl.when(not_last)
        def _():
            emb_copy(c).wait_recv()

            def add(i, carry):
                at = pl.ds(pl.multiple_of(c * part + i * 16, 16), 16)
                total = emb[at, :] + emb_recv[at, :].astype(jnp.float32)

                @pl.when(not_first)
                def _():
                    emb_send[at, :] = total.astype(jnp.bfloat16)

                @pl.when(sec == 0)
                def _():
                    angular = (
                        fields[at, 0:1] * angle_ref[0:1, :] + fields[at, 1:2] * angle_ref[1:2, :]
                    )
                    feat[me, at, :] = (total + angular).astype(jnp.bfloat16)

                return carry

            lax.fori_loop(0, part // 16, add, 0)

            @pl.when(not_first)
            def _():
                emb_copy(c).start()

            @pl.when(sec == 0)
            def _():
                gather_start(1, feat, c)

    def weight_grad(block):
        def step(t, carry):
            begin = pl.multiple_of(block * width + t * tile, tile)
            column = pl.ds(pl.multiple_of(t * tile, tile), tile)
            grad_w_ref[0, pl.ds(begin, tile), :] = lax.dot_general(
                stash[block, :, column], pre_grad[...], (((0,), (0,)), ((), ())),
                preferred_element_type=jnp.float32,
            ).astype(jnp.bfloat16)
            return carry

        lax.fori_loop(0, width // tile, step, 0)

    blocks = [me, partner]
    for j in range(1, chips):
        blocks += [at_chip(j, core), at_chip(j, 1 - core)]
    def rest():
        for c in range(CHUNKS // 2, CHUNKS):
            feed(c)
        for c in pieces[0]:
            gather_pass(0, stash, c)

    @pl.when(on_time)
    def _():
        backward(1)
        rest()
        weight_grad(blocks[0])

    chain(0)
    pl.when(late)(rest)
    for c in pieces[0]:
        gather_end(0, stash, c)
    for c in range(1, CHUNKS):
        @pl.when(on_time)
        def _():
            for b in blocks[1 + (c - 1) * (shards - 1) // (CHUNKS - 1) : 1 + c * (shards - 1) // (CHUNKS - 1)]:
                weight_grad(b)

        chain(c)

    @pl.when(sec == sections - 2)
    def _():
        grad_copy(CHUNKS - 1).start()

    @pl.when(on_time)
    def _():
        send_sums(2)
        send_sums(3)

    def forward(stop, c, carry):
        @pl.when(c + 1 < stop)
        def _():
            gather_pass(1, feat, c + 1)

        gather_end(1, feat, c)
        total = jnp.zeros((part, width), jnp.float32)
        for b in range(shards):
            total = total + jnp.dot(
                feat[b, moving(c), :], weight[b * width : (b + 1) * width, :],
                preferred_element_type=jnp.float32,
            )
        fwd_ref[0, moving(c), :] = gelu(total + bias_ref[...]).astype(jnp.bfloat16)
        return carry

    early = CHUNKS // 2

    @pl.when(late)
    def _():
        gather_pass(1, feat, 0)
        lax.fori_loop(0, early, functools.partial(forward, early), 0)
        backward(1)
        send_sums(2)
        send_sums(3)

        def every(block, carry):
            weight_grad(block)
            return carry

        lax.fori_loop(0, shards, every, 0)

    def total_grad(c):
        at = sum_rows(c)
        for j in range(1, chips):
            sum_copy(j, c).wait_recv()
        whole = own[0, at, :].astype(jnp.float32) + part_recv[0, at, :].astype(jnp.float32)
        for j in range(1, chips):
            whole = whole + x_recv[j - 1, at, :].astype(jnp.float32)
        grad_in_ref[0, at, :] = whole.astype(jnp.bfloat16)

    for h in range(2):
        part_copy(0, h).wait_recv()
    begin = jnp.where(late, early, 0)
    gather_pass(1, feat, begin)
    lax.fori_loop(begin, CHUNKS, functools.partial(forward, CHUNKS), 0)
    for c in range(3):
        total_grad(c)

    for g, buf in enumerate((stash, feat)):
        for c in pieces[g]:
            gather_drain(g, buf, c)
    for h in range(2):
        for j in range(chips):
            part_copy(j, h).wait_send()

    @pl.when(not_last)
    def _():
        for c in range(CHUNKS):
            act_copy(c).wait_send()

    @pl.when(not_first)
    def _():
        for c in range(CHUNKS):
            grad_copy(c).wait_send()
            emb_copy(c).wait_send()

    total_grad(3)
    for c in range(4):
        for j in range(1, chips):
            sum_copy(j, c).wait_send()


def store(pieces, fwd, grad_in, grad_w, grad_bias, fwd_out, grad_in_out, grad_w_out, grad_bias_out, sem):
    depth = grad_w.shape[1] // pieces
    copies = [(grad_w.at[0, pl.ds(i * depth, depth)], grad_w_out.at[0, pl.ds(i * depth, depth)]) for i in range(pieces)]
    copies += [(fwd, fwd_out), (grad_in, grad_in_out), (grad_bias, grad_bias_out)]
    copies = [pltpu.make_async_copy(src, dst, sem.at[i]) for i, (src, dst) in enumerate(copies)]
    for copy in copies:
        copy.start()
    for copy in copies:
        copy.wait()


def local(sections, shards, *args):
    args = list(args)
    rows, width = args[0].shape[1:]
    table_rows = args[6].shape[0]
    active = args[7].shape[1]
    for k in (7, 8, 9):
        args[k] = args[k].T
    wide = (table_rows + 127) // 128 * 128
    chips = shards // 2
    vmem = pl.BlockSpec(memory_space=pltpu.VMEM)
    hbm = pl.BlockSpec(memory_space=pltpu.HBM)
    dma = pltpu.SemaphoreType.DMA
    half, full = jnp.bfloat16, jnp.float32
    outs = (
        ((1, rows, width), half),
        ((1, rows, width), half),
        ((1, shards * width, width), half),
        ((1, width), full),
    )
    results = pl.pallas_call(
        functools.partial(kernel, sections, shards),
        out_shape=tuple(pltpu.VMEM(*out) for out in outs),
        in_specs=[hbm] * 12 + [pl.BlockSpec(memory_space=pltpu.SMEM)],
        out_specs=(vmem,) * 4,
        scratch_shapes=[
            pltpu.VMEM((2, rows, width), half),
            pltpu.VMEM((2, rows, width), half),
            pltpu.VMEM((shards * width, width), half),
            pltpu.VMEM((1, width), full),
            pltpu.VMEM((table_rows, width), half),
            pltpu.VMEM((active, rows), jnp.int32),
            pltpu.VMEM((active, rows), full),
            pltpu.VMEM((2, rows), full),
            pltpu.VMEM((2, width), full),
            pltpu.VMEM((rows, width), half),
            pltpu.VMEM((rows, active), jnp.int32),
            pltpu.VMEM((rows, active), full),
            pltpu.VMEM((rows, 8), full),
            pltpu.VMEM((shards, rows, width), half),
            pltpu.VMEM((shards, rows, width), half),
            pltpu.VMEM((rows, width), half),
            pltpu.VMEM((rows, wide), half),
            pltpu.VMEM((rows, width), full),
            pltpu.VMEM((rows, width), half),
            pltpu.VMEM((rows, width), half),
            pltpu.VMEM((rows, width), half),
            pltpu.VMEM((chips, rows, width), half),
            pltpu.VMEM((chips, rows, width), half),
            pltpu.VMEM((chips, rows, width), half),
            pltpu.VMEM((chips - 1, rows, width), half),
            dma((2,)),
            dma((9,)),
            dma((3, CHUNKS)),
            dma((3, CHUNKS)),
            dma((2, CHUNKS)),
            dma((2, CHUNKS)),
            dma((2, CHUNKS, chips - 1)),
            dma((2, CHUNKS, chips - 1)),
            dma((2, CHUNKS, chips - 1)),
            dma((2, CHUNKS, chips - 1)),
            dma((chips, 2)),
            dma((chips, 2)),
            dma((chips - 1, 4)),
            dma((chips - 1, 4)),
        ],
        compiler_params=pltpu.CompilerParams(
            collective_id=0, has_side_effects=True, vmem_limit_bytes=46 * 1024 * 1024
        ),
        cost_estimate=pl.CostEstimate(
            flops=6 * rows * shards * width * width, bytes_accessed=40 * rows * width, transcendentals=0
        ),
    )(*args)
    any_spec = pl.BlockSpec(memory_space=pl.ANY)
    return pl.pallas_call(
        functools.partial(store, 8),
        out_shape=tuple(jax.ShapeDtypeStruct(*out) for out in outs),
        in_specs=[any_spec] * 4,
        out_specs=(any_spec,) * 4,
        scratch_shapes=[dma((11,))],
        compiler_params=pltpu.CompilerParams(vmem_limit_bytes=1024 * 1024),
    )(*results)


def solution(mesh):
    return jax.shard_map(
        functools.partial(local, mesh.shape["section"], mesh.shape["fsdp"]),
        mesh=mesh,
        in_specs=(
            P("section", "groups", "fsdp"),
            P("section", "groups", "fsdp"),
            P("section", None, "groups", "fsdp"),
            P("section", None, "groups", "fsdp"),
            P("section", None, "fsdp"),
            P("section", "fsdp"),
            P("section", "fsdp"),
            P("groups", None),
            P("groups", None),
            P("groups", None),
            P(None, "fsdp"),
            P("groups", "fsdp"),
            P("section"),
        ),
        out_specs=(
            P("section", "groups", "fsdp"),
            P("section", "groups", "fsdp"),
            P("section", "groups", "fsdp"),
            P("section", ("groups", "fsdp")),
        ),
        check_vma=False,
    )
```
